512 devices in a mesh: dp: 8 (over y_hi, x), expert: 64 (over y_lo, z, core).
Axes of the slice: x: 4, y: 8 (y_hi: 2, y_lo: 4; y = y_hi * 4 + y_lo), z: 8, core: 2. Of those that a mesh axis runs over, the one named last changes fastest.
Arguments:
- tokens: bfloat16 [65536, 2560], P(('dp', 'expert')), may hold values from -6 to 6
- expert_ids: int32 [65536, 6], P(('dp', 'expert')), may hold values from 0 to 159, as said below
- gate_probs: float32 [65536, 6], P(('dp', 'expert')), may hold values from 0.1 to 1
- act_grad: bfloat16 [65536, 6, 1024], P(('dp', 'expert')), may hold values from -0.59765625 to 0.59765625
- hot_experts: int32 [32], replicated, may hold values from 0 to 63, as said below
- w_gate: bfloat16 [64, 2560, 1024], P('expert', None, 'dp'), may hold values from -0.125 to 0.125
- w_up: bfloat16 [64, 2560, 1024], P('expert', None, 'dp'), may hold values from -0.125 to 0.125
Outputs:
- grad_gate: bfloat16 [64, 2560, 1024], P('expert', None, 'dp')
- grad_up: bfloat16 [64, 2560, 1024], P('expert', None, 'dp')
The draws below stay inside these ranges and needn't reach their ends.
Inputs may be any that keep to these rules, and one draw needn't show every extreme that they name: `expert_ids`: each row names 6 different experts. `hot_experts`: 32 different experts, always including 0, 1, 30, 31, 32, 33, 62 and 63.
All inputs are finite; a program needn't handle non-finite values.
Results may differ from the reference program's by a relative error of at most 0.0061.
Values may be sent and summed in bfloat16 or wider, within the bound.
No kernel may reach another device: no remote copies, remote signals or barrier semaphores. Data moves between devices by JAX's collectives and lax.ppermute only.
A program may use at most 128 MiB of HBM per device.

```python
import jax
import jax.numpy as jnp
from jax import lax

D = 2560
FF = 1024
SPECIALIST_COUNT = 160
TOP = 6
CAP = 2
OVF = 2
TOK_DEV = 128
EXPERTS = 64
HOT = 32
TOKENS = 65536


def hot_choice(key):
    scores = jax.random.randint(jax.random.fold_in(key, 101), (EXPERTS,), 0, 100000, dtype=jnp.int32)
    scores = scores * EXPERTS + jnp.arange(EXPERTS, dtype=jnp.int32)
    needed = jnp.array([0, 1, EXPERTS // 2 - 2, EXPERTS // 2 - 1, EXPERTS // 2, EXPERTS // 2 + 1, EXPERTS - 2, EXPERTS - 1], jnp.int32)
    boost = jnp.zeros((EXPERTS,), jnp.int32).at[needed].set(100000 * EXPERTS)
    picked = lax.top_k(scores + boost, HOT)[1]
    return picked.astype(jnp.int32)


def draw_hot_experts(key, part):
    return hot_choice(key)


def draw_expert_ids(key, part):
    favoured_specialists = hot_choice(key)
    drawn_logits = jax.random.randint(jax.random.fold_in(key, 202), (TOKENS, SPECIALIST_COUNT), 0, 1000, dtype=jnp.int32)
    favour_increment = jnp.zeros((SPECIALIST_COUNT,), jnp.int32).at[favoured_specialists].set(250)
    router_logits = (drawn_logits + favour_increment[None, :]) * 256 + jnp.arange(SPECIALIST_COUNT, dtype=jnp.int32)[None, :]
    chosen = lax.top_k(router_logits, TOP)[1]
    return chosen.astype(jnp.int32)


def shard_levels(rng, shape, cuts, smallest, top_value):
    loudness, own = 1.0, jax.random.fold_in(rng, 6)
    for axis_at, shards_of in cuts:
        heights = jnp.exp(jax.random.uniform(jax.random.fold_in(own, axis_at), (shards_of,), jnp.float32, smallest / len(cuts), top_value / len(cuts)))
        loudness = loudness * jnp.repeat(heights, shape[axis_at] // shards_of).reshape([-1 if axis == axis_at else 1 for axis in range(len(shape))])
    return loudness


def gaussian(key, dims, spread, limit, cuts=(), kind=jnp.bfloat16):
    values = jax.random.normal(key, dims, jnp.float32) * spread
    if len(cuts) > 0:
        values = shard_levels(key, dims, cuts, -0.22, 0.18) * values
    return jnp.clip(values, min=-limit, max=limit).astype(kind)


def setup_inputs(seed: int = 0) -> dict:
    keys = jax.random.split(jax.random.key(seed), 8)
    return {
        "tokens": gaussian(keys[0], (TOKENS, D), 1.0, 6.0, ((0, 512),)),
        "expert_ids": draw_expert_ids(jax.random.fold_in(keys[7], 71), 0),
        "gate_probs": jnp.clip(0.1 + 0.9 * jax.random.uniform(keys[2], (TOKENS, TOP), jnp.float32) ** shard_levels(keys[2], (TOKENS, TOP), ((0, 512),), -0.2, 0.2), 0.1, 1.0),
        "act_grad": gaussian(keys[3], (TOKENS, TOP, FF), 0.1, 0.59765625, ((0, 512),)),
        "hot_experts": draw_hot_experts(jax.random.fold_in(keys[7], 71), 0),
        "w_gate": gaussian(keys[5], (EXPERTS, D, FF), D ** -0.5, 0.125, ((0, 64), (2, 8))),
        "w_up": gaussian(keys[6], (EXPERTS, D, FF), D ** -0.5, 0.125, ((0, 64), (2, 8))),
    }


def expert_grads(tok_rows, act_rows, weight_gate, weight_up):
    gate_pre = jnp.dot(tok_rows, weight_gate, preferred_element_type=jnp.float32)
    up_pre = jnp.dot(tok_rows, weight_up, preferred_element_type=jnp.float32)
    sigma_gate = jax.nn.sigmoid(gate_pre)
    upstream = act_rows.astype(jnp.float32)
    grad_up_rows = (upstream * gate_pre * sigma_gate).astype(jnp.bfloat16)
    grad_gate_rows = (upstream * up_pre * sigma_gate * (1.0 + gate_pre * (1.0 - sigma_gate))).astype(jnp.bfloat16)
    contract = (((0,), (0,)), ((), ()))
    gate_sum = lax.dot_general(tok_rows, grad_gate_rows, contract, preferred_element_type=jnp.float32)
    up_gradient_sum = lax.dot_general(tok_rows, grad_up_rows, contract, preferred_element_type=jnp.float32)
    return gate_sum, up_gradient_sum


def block_positions(block_ids):
    matching = block_ids[:, None] == jnp.arange(EXPERTS, dtype=jnp.int32)[None, :]
    running = jnp.cumsum(matching.astype(jnp.int32), axis=0) - 1
    return jnp.sum(jnp.where(matching, running, 0), axis=1).astype(jnp.int32)


def reference(tokens, expert_ids, gate_probs, act_grad, hot_experts, w_gate, w_up):
    blocks = TOKENS // TOK_DEV
    per_block = TOK_DEV * TOP
    block_ids = expert_ids.reshape(blocks, per_block).astype(jnp.int32)
    position = jax.vmap(block_positions)(block_ids)
    in_window = block_ids < EXPERTS
    is_popular = jnp.any(block_ids[:, :, None] == hot_experts[None, None, :], axis=2)
    own_mask = in_window & (position < CAP)
    lent_mask = in_window & is_popular & (position >= CAP) & (position < CAP + OVF)
    numbers = jnp.arange(blocks * per_block, dtype=jnp.int32).reshape(blocks, per_block)
    block_index = jnp.arange(blocks, dtype=jnp.int32)[:, None]
    own_slot = jnp.where(own_mask, (block_ids * blocks + block_index) * CAP + position, EXPERTS * blocks * CAP).astype(jnp.int32)
    own_table = jnp.full((EXPERTS * blocks * CAP,), -1, jnp.int32).at[own_slot.reshape(-1)].set(numbers.reshape(-1), mode="drop")
    own_table = own_table.reshape(EXPERTS, blocks * CAP)
    lent_slot = jnp.where(lent_mask, (block_ids * blocks + block_index) * OVF + position - CAP, EXPERTS * blocks * OVF).astype(jnp.int32)
    lent_table = jnp.full((EXPERTS * blocks * OVF,), -1, jnp.int32).at[lent_slot.reshape(-1)].set(numbers.reshape(-1), mode="drop")
    lent_table = lent_table.reshape(EXPERTS, blocks * OVF)
    flat_acts = act_grad.reshape(-1, FF)
    flat_probs = gate_probs.reshape(-1)

    def partial_sums(table, weight_gate, weight_up):
        valid = table >= 0
        index = jnp.maximum(table, 0).astype(jnp.int32)
        tok_rows = jnp.where(valid[:, None], tokens[index // TOP], jnp.zeros((), tokens.dtype))
        act_rows = (flat_probs[index][:, None] * flat_acts[index].astype(jnp.float32)).astype(jnp.bfloat16)
        act_rows = jnp.where(valid[:, None], act_rows, jnp.zeros((), act_rows.dtype))
        return expert_grads(tok_rows, act_rows, weight_gate, weight_up)

    def one_expert(inputs):
        own_rows, lent_rows, weight_gate, weight_up = inputs
        own_gate, own_up = partial_sums(own_rows, weight_gate, weight_up)
        lent_gate, lent_up = partial_sums(lent_rows, weight_gate, weight_up)
        lent_gate = lax.optimization_barrier(lent_gate.astype(jnp.bfloat16)).astype(jnp.float32)
        lent_up = lax.optimization_barrier(lent_up.astype(jnp.bfloat16)).astype(jnp.float32)
        return ((own_gate + lent_gate).astype(jnp.bfloat16), (own_up + lent_up).astype(jnp.bfloat16))

    grad_gate, grad_up = lax.map(one_expert, (own_table, lent_table, w_gate, w_up))
    return grad_gate, grad_up
```

```python
import jax
import jax.numpy as jnp
from jax import lax
from jax.experimental import pallas as pl
from jax.experimental.pallas import tpu as pltpu
from jax.sharding import Mesh, PartitionSpec as P

CAP = 2
OVF = 2
SLOTS = CAP + OVF
AXES = ("yh", "x", "yl", "z", "c")
PLANE = ("yh", "yl", "z", "c")
EXPERT = ("yl", "z", "c")


def pack_kernel(ids_ref, probs_ref, hot_ref, tok_ref, act_ref, out_ref):
    top, block = ids_ref.shape
    experts = out_ref.shape[1] // SLOTS
    rows = experts * SLOTS
    width = tok_ref.shape[1]
    half = out_ref.shape[2] - width
    row = lax.broadcasted_iota(jnp.int32, (rows, block), 0)
    expert, slot = row // SLOTS, row % SLOTS
    hits = [ids_ref[k : k + 1, :] == expert for k in range(top)]
    named = hits[0]
    for hit in hits[1:]:
        named = named | hit
    before = lax.broadcasted_iota(jnp.int32, (block, block), 0) < lax.broadcasted_iota(
        jnp.int32, (block, block), 1
    )
    position = jnp.dot(
        jnp.where(named, 1.0, 0.0).astype(jnp.bfloat16),
        jnp.where(before, 1.0, 0.0).astype(jnp.bfloat16),
        preferred_element_type=jnp.float32,
    ).astype(jnp.int32)
    hots = hot_ref.shape[1]
    owner = lax.broadcasted_iota(jnp.int32, (rows, hots), 0) // SLOTS
    hot = jnp.max(jnp.where(hot_ref[...] == owner, 1, 0), axis=1, keepdims=True)
    kept = named & (position == slot) & ((slot < CAP) | (hot > 0))
    pick = jnp.where(kept, 1.0, 0.0).astype(jnp.bfloat16)
    toks = jnp.dot(pick, tok_ref[...], preferred_element_type=jnp.float32)
    toks = toks.astype(jnp.bfloat16)
    out_ref[0, :, :width] = toks
    out_ref[1, :, :width] = toks
    acts = jnp.zeros((rows, act_ref.shape[2]), jnp.float32)
    for k in range(top):
        scaled = (probs_ref[:, k : k + 1] * act_ref[k].astype(jnp.float32)).astype(jnp.bfloat16)
        chosen = jnp.where(kept & hits[k], 1.0, 0.0).astype(jnp.bfloat16)
        acts += jnp.dot(chosen, scaled, preferred_element_type=jnp.float32)
    acts = acts.astype(jnp.bfloat16)
    out_ref[0, :, width:] = acts[:, :half]
    out_ref[1, :, width:] = acts[:, half:]


def body(tokens, expert_ids, gate_probs, act_grad, hot_experts, w_gate, w_up):
    width = tokens.shape[1]
    ff = act_grad.shape[2]
    copies = lax.axis_size("yh")
    experts = lax.axis_size(EXPERT)
    wg = lax.all_gather(w_gate[0], "x", axis=0)
    wu = lax.all_gather(w_up[0], "x", axis=0)
    send = pl.pallas_call(
        pack_kernel,
        out_shape=jax.ShapeDtypeStruct(
            (copies, experts * SLOTS, width + ff // copies), jnp.bfloat16
        ),
        compiler_params=pltpu.CompilerParams(vmem_limit_bytes=40 * 2**20),
        name="pack_rows",
    )(
        expert_ids.T,
        gate_probs,
        hot_experts.reshape(1, -1),
        tokens,
        jnp.swapaxes(act_grad, 0, 1),
    )
    send = send.reshape(copies * experts, SLOTS, -1)
    recv = lax.all_to_all(send, PLANE, 0, 0, tiled=True)
    recv = recv.reshape(copies * experts * SLOTS, -1)
    toks = recv[:, :width]
    upstream = recv[:, width:].astype(jnp.float32)
    wg = jnp.swapaxes(wg, 0, 1).reshape(width, -1)
    wu = jnp.swapaxes(wu, 0, 1).reshape(width, -1)
    gate = jnp.dot(toks, wg, preferred_element_type=jnp.float32)
    up = jnp.dot(toks, wu, preferred_element_type=jnp.float32)
    sig = jax.nn.sigmoid(gate)
    d_up = (upstream * gate * sig).astype(jnp.bfloat16)
    d_gate = (upstream * up * sig * (1.0 + gate * (1.0 - sig))).astype(jnp.bfloat16)
    planes = lax.axis_size("x")
    parts = []
    for d in (d_gate, d_up):
        total = lax.dot_general(
            toks, d, (((0,), (0,)), ((), ())), preferred_element_type=jnp.float32
        )
        parts.append(jnp.swapaxes(total.astype(jnp.bfloat16).reshape(width, planes, -1), 0, 1))
    parts = jnp.stack(parts, 1)
    out = lax.psum_scatter(parts, "x", scatter_dimension=0, tiled=True)[0]
    return (out[0:1], out[1:2])


def solution(mesh):
    grid = Mesh(mesh.devices.reshape(2, 4, 4, 8, 2), AXES)
    rows = P(AXES)
    weights = P(EXPERT, None, ("yh", "x"))
    return jax.shard_map(
        body,
        mesh=grid,
        in_specs=(rows, rows, rows, rows, P(), weights, weights),
        out_specs=(weights, weights),
        check_vma=False,
    )
```

```python
import jax
import jax.numpy as jnp
from jax import lax
from jax.experimental import pallas as pl
from jax.experimental.pallas import tpu as pltpu
from jax.sharding import Mesh, PartitionSpec as P

CAP = 2
OVF = 2
SLOTS = CAP + OVF
AXES = ("yh", "x", "yl", "z", "c")
PLANE = ("yh", "yl", "z", "c")
EXPERT = ("yl", "z", "c")


def pack_kernel(ids_ref, probs_ref, hot_ref, tok_ref, act_ref, out_ref):
    top, block = ids_ref.shape
    experts = out_ref.shape[1] // SLOTS
    rows = experts * SLOTS
    width = tok_ref.shape[1]
    half = out_ref.shape[2] - width
    row = lax.broadcasted_iota(jnp.int32, (rows, block), 0)
    expert, slot = row // SLOTS, row % SLOTS
    hits = [ids_ref[k : k + 1, :] == expert for k in range(top)]
    named = hits[0]
    for hit in hits[1:]:
        named = named | hit
    before = lax.broadcasted_iota(jnp.int32, (block, block), 0) < lax.broadcasted_iota(
        jnp.int32, (block, block), 1
    )
    position = jnp.dot(
        jnp.where(named, 1.0, 0.0).astype(jnp.bfloat16),
        jnp.where(before, 1.0, 0.0).astype(jnp.bfloat16),
        preferred_element_type=jnp.float32,
    ).astype(jnp.int32)
    hots = hot_ref.shape[1]
    owner = lax.broadcasted_iota(jnp.int32, (rows, hots), 0) // SLOTS
    hot = jnp.max(jnp.where(hot_ref[...] == owner, 1, 0), axis=1, keepdims=True)
    kept = named & (position == slot) & ((slot < CAP) | (hot > 0))
    pick = jnp.where(kept, 1.0, 0.0).astype(jnp.bfloat16)
    toks = jnp.dot(pick, tok_ref[...], preferred_element_type=jnp.float32)
    toks = toks.astype(jnp.bfloat16)
    out_ref[0, :, :width] = toks
    out_ref[1, :, :width] = toks
    acts = jnp.zeros((rows, act_ref.shape[2]), jnp.float32)
    for k in range(top):
        scaled = (probs_ref[:, k : k + 1] * act_ref[k].astype(jnp.float32)).astype(jnp.bfloat16)
        chosen = jnp.where(kept & hits[k], 1.0, 0.0).astype(jnp.bfloat16)
        acts += jnp.dot(chosen, scaled, preferred_element_type=jnp.float32)
    acts = acts.astype(jnp.bfloat16)
    out_ref[0, :, width:] = acts[:, :half]
    out_ref[1, :, width:] = acts[:, half:]


def slice_kernel(which_ref, rows_ref, act_ref, wg_ref, wu_ref, gate_ref, up_ref):
    hidden = act_ref.shape[1]
    toks = rows_ref[...]
    pair = jnp.concatenate([wg_ref[0], wu_ref[0]], axis=1)
    both = jnp.dot(toks, pair, preferred_element_type=jnp.float32)
    gate, up = both[:, :hidden], both[:, hidden:]
    upstream = act_ref[...].astype(jnp.float32)
    sig = 1.0 / (1.0 + jnp.exp(-gate))
    d_up = upstream * gate * sig
    d_gate = upstream * up * sig * (1.0 + gate * (1.0 - sig))
    d = jnp.concatenate([d_gate, d_up], axis=1).astype(jnp.bfloat16)
    total = lax.dot_general(
        toks, d, (((0,), (0,)), ((), ())), preferred_element_type=jnp.float32
    )
    gate_ref[0] = total[:, :hidden].astype(gate_ref.dtype)
    up_ref[0] = total[:, hidden:].astype(up_ref.dtype)


def slice_grads(which, recv, wg, wu, dtype):
    rows, columns = recv.shape
    _, width, hidden = wg.shape
    return pl.pallas_call(
        slice_kernel,
        grid_spec=pltpu.PrefetchScalarGridSpec(
            num_scalar_prefetch=1,
            grid=(1,),
            in_specs=[
                pl.BlockSpec((rows, width), lambda i, w: (0, 0)),
                pl.BlockSpec((rows, hidden), lambda i, w: (0, width // hidden + w[0])),
                pl.BlockSpec((1, width, hidden), lambda i, w: (w[0], 0, 0)),
                pl.BlockSpec((1, width, hidden), lambda i, w: (w[0], 0, 0)),
            ],
            out_specs=[pl.BlockSpec((1, width, hidden), lambda i, w: (0, 0, 0))] * 2,
        ),
        out_shape=[jax.ShapeDtypeStruct((1, width, hidden), dtype)] * 2,
        compiler_params=pltpu.CompilerParams(vmem_limit_bytes=48 * 2**20),
        cost_estimate=pl.CostEstimate(
            flops=8 * rows * width * hidden,
            bytes_accessed=2 * rows * width + 8 * width * hidden,
            transcendentals=rows * hidden,
        ),
        name="slice_grads",
    )(which.reshape(1), recv, recv, wg, wu)


def moved(block, distance):
    planes = lax.axis_size("x")
    return lax.ppermute(block, "x", [(i, (i + distance) % planes) for i in range(planes)])


def add(*blocks):
    return sum(block.astype(jnp.float32) for block in blocks)


def body(tokens, expert_ids, gate_probs, act_grad, hot_experts, w_gate, w_up):
    width = tokens.shape[1]
    ff = act_grad.shape[2]
    copies = lax.axis_size("yh")
    experts = lax.axis_size(EXPERT)
    planes = lax.axis_size("x")
    here = lax.axis_index("x")
    wg = lax.all_gather(w_gate[0], "x", axis=0)
    wu = lax.all_gather(w_up[0], "x", axis=0)
    send = pl.pallas_call(
        pack_kernel,
        out_shape=jax.ShapeDtypeStruct(
            (copies, experts * SLOTS, width + ff // copies), jnp.bfloat16
        ),
        compiler_params=pltpu.CompilerParams(vmem_limit_bytes=40 * 2**20),
        name="pack_rows",
    )(
        expert_ids.T,
        gate_probs,
        hot_experts.reshape(1, -1),
        tokens,
        jnp.swapaxes(act_grad, 0, 1),
    )
    send = send.reshape(copies * experts, SLOTS, -1)
    recv = lax.all_to_all(send, PLANE, 0, 0, tiled=True)
    recv = recv.reshape(copies * experts * SLOTS, -1)

    def part(offset, dtype=jnp.bfloat16):
        return slice_grads((here + offset) % planes, recv, wg, wu, dtype)

    far_gate, far_up = part(2)
    far_gate = moved(far_gate, 1)
    far_up = moved(far_up, -1)
    right_gate, right_up = part(1)
    from_left_up = moved(right_up, 1)
    left_gate, left_up = part(3)
    from_right_gate = moved(left_gate, -1)
    own_gate, own_up = part(0, jnp.float32)
    from_left_gate = moved(add(right_gate, far_gate).astype(jnp.bfloat16), 1)
    from_right_up = moved(add(left_up, far_up).astype(jnp.bfloat16), -1)
    grad_gate = add(own_gate, from_right_gate, from_left_gate)
    grad_up = add(own_up, from_left_up, from_right_up)
    return (grad_gate.astype(jnp.bfloat16), grad_up.astype(jnp.bfloat16))


def solution(mesh):
    grid = Mesh(mesh.devices.reshape(2, 4, 4, 8, 2), AXES)
    rows = P(AXES)
    weights = P(EXPERT, None, ("yh", "x"))
    return jax.shard_map(
        body,
        mesh=grid,
        in_specs=(rows, rows, rows, rows, P(), weights, weights),
        out_specs=(weights, weights),
        check_vma=False,
    )
```

```python
import functools

import jax
import jax.numpy as jnp
from jax import lax
from jax.experimental import pallas as pl
from jax.experimental.pallas import tpu as pltpu
from jax.sharding import Mesh, PartitionSpec as P

CAP = 2
OVF = 2
SLOTS = CAP + OVF
VMEM = 60 * 2**20
SLICE_VMEM = 60 * 2**20
AXES = ("yh", "x", "yl", "z", "c")
PLANE = ("yh", "yl", "z", "c")
EXPERT = ("yl", "z", "c")


def pack_kernel(ids_ref, probs_ref, hot_ref, tok_ref, act_ref, out_ref):
    top, block = ids_ref.shape
    experts = out_ref.shape[0] // 2
    rows = experts * SLOTS
    width = tok_ref.shape[1]
    half = out_ref.shape[2] - width
    row = lax.broadcasted_iota(jnp.int32, (rows, block), 0)
    expert, slot = row // SLOTS, row % SLOTS
    hits = [ids_ref[k : k + 1, :] == expert for k in range(top)]
    named = hits[0]
    for hit in hits[1:]:
        named = named | hit
    before = lax.broadcasted_iota(jnp.int32, (block, block), 0) < lax.broadcasted_iota(
        jnp.int32, (block, block), 1
    )
    position = jnp.dot(
        jnp.where(named, 1.0, 0.0).astype(jnp.bfloat16),
        jnp.where(before, 1.0, 0.0).astype(jnp.bfloat16),
        preferred_element_type=jnp.float32,
    ).astype(jnp.int32)
    hots = hot_ref.shape[1]
    owner = lax.broadcasted_iota(jnp.int32, (rows, hots), 0) // SLOTS
    hot = jnp.max(jnp.where(hot_ref[...] == owner, 1, 0), axis=1, keepdims=True)
    kept = named & (position == slot) & ((slot < CAP) | (hot > 0))
    pick = jnp.where(kept, 1.0, 0.0).astype(jnp.bfloat16)
    toks = jnp.dot(pick, tok_ref[...], preferred_element_type=jnp.float32)
    toks = toks.astype(jnp.bfloat16).reshape(experts, SLOTS, width)
    out_ref[:experts, :, :width] = toks
    out_ref[experts:, :, :width] = toks
    acts = jnp.zeros((rows, act_ref.shape[2]), jnp.float32)
    scale = jnp.zeros((rows, block), jnp.float32)
    for k in range(top):
        chosen = jnp.where(kept & hits[k], 1.0, 0.0)
        acts += jnp.dot(chosen.astype(jnp.bfloat16), act_ref[k], preferred_element_type=jnp.float32)
        scale += chosen * probs_ref[k : k + 1, :]
    acts = jnp.sum(scale, axis=1, keepdims=True) * acts
    acts = acts.astype(jnp.bfloat16)
    out_ref[:experts, :, width:] = acts[:, :half].reshape(experts, SLOTS, half)
    out_ref[experts:, :, width:] = acts[:, half:].reshape(experts, SLOTS, half)


def pre_grads(toks, act, w_gate, w_up):
    hidden = act.shape[1]
    pair = jnp.concatenate([w_gate, w_up], axis=1)
    both = jnp.dot(toks, pair, preferred_element_type=jnp.float32)
    gate, up = both[:, :hidden], both[:, hidden:]
    upstream = act.astype(jnp.float32)
    sig = 1.0 / (1.0 + jnp.exp(-gate))
    d_up = upstream * gate * sig
    d_gate = upstream * up * sig * (1.0 + gate * (1.0 - sig))
    return jnp.concatenate([d_gate, d_up], axis=1).astype(jnp.bfloat16)


def store_grads(toks, d, gate_ref, up_ref):
    hidden = gate_ref.shape[2]
    total = lax.dot_general(
        toks, d, (((0,), (0,)), ((), ())), preferred_element_type=jnp.float32
    )
    gate_ref[0] = total[:, :hidden].astype(gate_ref.dtype)
    up_ref[0] = total[:, hidden:].astype(up_ref.dtype)


CHUNKS = 4


def slices_kernel(count, which_ref, recv_ref, *refs):
    weights, grads, (rows, sems) = refs[: 2 * count], refs[2 * count : -2], refs[-2:]
    width, hidden = weights[0].shape[1:]
    chunk = rows.shape[0] // CHUNKS
    parts = [pl.ds(c * chunk, chunk) for c in range(CHUNKS)]
    copies = [
        pltpu.make_async_copy(recv_ref.at[part], rows.at[part], sems.at[c])
        for c, part in enumerate(parts)
    ]
    for copy in copies:
        copy.start()
    d = [[] for _ in range(count)]
    for part, copy in zip(parts, copies):
        copy.wait()
        for k in range(count):
            start = pl.multiple_of(width + which_ref[k] * hidden, hidden)
            d[k].append(
                pre_grads(
                    rows[part, :width],
                    rows[part, pl.ds(start, hidden)],
                    weights[2 * k][0],
                    weights[2 * k + 1][0],
                )
            )
    for k in range(count):
        store_grads(rows[:, :width], jnp.concatenate(d[k]), *grads[2 * k : 2 * k + 2])


def slice_grads(which, recv, weights, dtype):
    shape = weights[0].shape
    w_size = weights[0].size * len(weights) // 2
    whole = pl.BlockSpec(shape, lambda i, w: (0, 0, 0))
    return pl.pallas_call(
        functools.partial(slices_kernel, len(weights) // 2),
        grid_spec=pltpu.PrefetchScalarGridSpec(
            num_scalar_prefetch=1,
            grid=(1,),
            in_specs=[pl.BlockSpec(memory_space=pl.ANY)] + [whole] * len(weights),
            out_specs=[whole] * len(weights),
            scratch_shapes=[
                pltpu.VMEM(recv.shape, recv.dtype),
                pltpu.SemaphoreType.DMA((CHUNKS,)),
            ],
        ),
        out_shape=[jax.ShapeDtypeStruct(shape, dtype)] * len(weights),
        compiler_params=pltpu.CompilerParams(vmem_limit_bytes=SLICE_VMEM),
        cost_estimate=pl.CostEstimate(
            flops=8 * recv.shape[0] * w_size,
            bytes_accessed=2 * recv.size + 8 * w_size,
            transcendentals=0,
        ),
        name="slice_grads",
    )(which, recv, *weights)


def moved(block, distance):
    planes = lax.axis_size("x")
    return lax.ppermute(block, "x", [(i, (i + distance) % planes) for i in range(planes)])


def add(*blocks):
    return sum(block.astype(jnp.float32) for block in blocks)


def body(tokens, expert_ids, gate_probs, act_grad, hot_experts, w_gate, w_up):
    width = tokens.shape[1]
    ff = act_grad.shape[2]
    copies = lax.axis_size("yh")
    experts = lax.axis_size(EXPERT)
    planes = lax.axis_size("x")
    here = lax.axis_index("x")
    send = pl.pallas_call(
        pack_kernel,
        out_shape=jax.ShapeDtypeStruct(
            (copies * experts, SLOTS, width + ff // copies), jnp.bfloat16
        ),
        compiler_params=pltpu.CompilerParams(vmem_limit_bytes=VMEM),
        name="pack_rows",
    )(
        expert_ids.T,
        gate_probs.T,
        hot_experts.reshape(1, -1),
        tokens,
        jnp.swapaxes(act_grad, 0, 1),
    )
    send, w_gate, w_up = lax.optimization_barrier((send, w_gate, w_up))
    recv = lax.all_to_all(send, PLANE, 0, 0, tiled=True)
    mine = (w_gate, w_up)
    theirs = {d: tuple(moved(w, -d) for w in mine) for d in (2, 1, 3)}
    at = jnp.stack([(here + d) % planes for d in range(planes)])

    recv, theirs = lax.optimization_barrier((recv.reshape(-1, recv.shape[2]), theirs))
    far_gate, far_up = slice_grads(at[2:3], recv, theirs[2], jnp.bfloat16)
    far_gate = moved(far_gate, 1)
    far_up = moved(far_up, -1)
    right_gate, right_up, left_gate, left_up = slice_grads(
        at[1::2], recv, theirs[1] + theirs[3], jnp.bfloat16
    )
    from_left_up = moved(right_up, 1)
    from_right_gate = moved(left_gate, -1)
    own_gate, own_up = slice_grads(at[0:1], recv, mine, jnp.float32)
    from_left_gate = moved(add(right_gate, far_gate).astype(jnp.bfloat16), 1)
    from_right_up = moved(add(left_up, far_up).astype(jnp.bfloat16), -1)
    grad_gate = add(own_gate, from_right_gate, from_left_gate)
    grad_up = add(own_up, from_left_up, from_right_up)
    return (grad_gate.astype(jnp.bfloat16), grad_up.astype(jnp.bfloat16))


def solution(mesh):
    grid = Mesh(mesh.devices.reshape(2, 4, 4, 8, 2), AXES)
    rows = P(AXES)
    weights = P(EXPERT, None, ("yh", "x"))
    return jax.shard_map(
        body,
        mesh=grid,
        in_specs=(rows, rows, rows, rows, P(), weights, weights),
        out_specs=(weights, weights),
        check_vma=False,
    )
```

```python
import functools

import jax
import jax.numpy as jnp
from jax import lax
from jax.experimental import pallas as pl
from jax.experimental.pallas import tpu as pltpu
from jax.sharding import Mesh, PartitionSpec as P

CAP = 2
OVF = 2
SLOTS = CAP + OVF
VMEM = 60 * 2**20
SLICE_VMEM = 60 * 2**20
AXES = ("yh", "x", "yl", "z", "c")
PLANE = ("yh", "yl", "z", "c")
EXPERT = ("yl", "z", "c")


def pack_kernel(ids_ref, probs_ref, hot_ref, tok_ref, act_ref, out_ref):
    top, block = ids_ref.shape
    experts = out_ref.shape[0] // 2
    rows = experts * SLOTS
    width = tok_ref.shape[1]
    half = out_ref.shape[2] - width
    row = lax.broadcasted_iota(jnp.int32, (rows, block), 0)
    expert, slot = row // SLOTS, row % SLOTS
    hits = [ids_ref[k : k + 1, :] == expert for k in range(top)]
    named = hits[0]
    for hit in hits[1:]:
        named = named | hit
    before = lax.broadcasted_iota(jnp.int32, (block, block), 0) < lax.broadcasted_iota(
        jnp.int32, (block, block), 1
    )
    position = jnp.dot(
        jnp.where(named, 1.0, 0.0).astype(jnp.bfloat16),
        jnp.where(before, 1.0, 0.0).astype(jnp.bfloat16),
        preferred_element_type=jnp.float32,
    ).astype(jnp.int32)
    hots = hot_ref.shape[1]
    owner = lax.broadcasted_iota(jnp.int32, (rows, hots), 0) // SLOTS
    hot = jnp.max(jnp.where(hot_ref[...] == owner, 1, 0), axis=1, keepdims=True)
    kept = named & (position == slot) & ((slot < CAP) | (hot > 0))
    pick = jnp.where(kept, 1.0, 0.0).astype(jnp.bfloat16)
    toks = jnp.dot(pick, tok_ref[...], preferred_element_type=jnp.float32)
    toks = toks.astype(jnp.bfloat16).reshape(experts, SLOTS, width)
    out_ref[:experts, :, :width] = toks
    out_ref[experts:, :, :width] = toks
    acts = jnp.zeros((rows, act_ref.shape[2]), jnp.float32)
    scale = jnp.zeros((rows, block), jnp.float32)
    for k in range(top):
        chosen = jnp.where(kept & hits[k], 1.0, 0.0)
        acts += jnp.dot(chosen.astype(jnp.bfloat16), act_ref[k], preferred_element_type=jnp.float32)
        scale += chosen * probs_ref[k : k + 1, :]
    acts = jnp.sum(scale, axis=1, keepdims=True) * acts
    acts = acts.astype(jnp.bfloat16)
    out_ref[:experts, :, width:] = acts[:, :half].reshape(experts, SLOTS, half)
    out_ref[experts:, :, width:] = acts[:, half:].reshape(experts, SLOTS, half)


def pre_grads(gate, up, act):
    upstream = act.astype(jnp.float32)
    sig = 1.0 / (1.0 + jnp.exp(-gate))
    d_up = upstream * gate * sig
    d_gate = upstream * up * sig * (1.0 + gate * (1.0 - sig))
    return [d_gate.astype(jnp.bfloat16), d_up.astype(jnp.bfloat16)]


CHUNKS = 2
TILES = 5


def slices_kernel(count, which_ref, recv_ref, *refs):
    weights, grads, (rows, sems) = refs[: 2 * count], refs[2 * count : -2], refs[-2:]
    width, hidden = weights[0].shape[1:]
    chunk = rows.shape[0] // CHUNKS
    parts = [pl.ds(c * chunk, chunk) for c in range(CHUNKS)]
    copies = [
        pltpu.make_async_copy(recv_ref.at[part], rows.at[part], sems.at[c])
        for c, part in enumerate(parts)
    ]
    for copy in copies:
        copy.start()
    d = []
    for part, copy in zip(parts, copies):
        copy.wait()
        row = []
        for k in range(count):
            pair = jnp.concatenate([weights[2 * k][0], weights[2 * k + 1][0]], axis=1)
            both = jnp.dot(rows[part, :width], pair, preferred_element_type=jnp.float32)
            start = pl.multiple_of(width + which_ref[k] * hidden, hidden)
            row += pre_grads(both[:, :hidden], both[:, hidden:], rows[part, pl.ds(start, hidden)])
        d.append(jnp.concatenate(row, axis=1))
    d = jnp.concatenate(d)
    tile = width // TILES
    for t in range(TILES):
        cols = slice(t * tile, (t + 1) * tile)
        total = lax.dot_general(
            rows[:, cols], d, (((0,), (0,)), ((), ())), preferred_element_type=jnp.float32
        )
        for k, ref in enumerate(grads):
            ref[0, cols, :] = total[:, k * hidden : (k + 1) * hidden].astype(ref.dtype)


def slice_grads(which, recv, weights, dtype):
    shape = weights[0].shape
    w_size = weights[0].size * len(weights) // 2
    whole = pl.BlockSpec(shape, lambda i, w: (0, 0, 0))
    return pl.pallas_call(
        functools.partial(slices_kernel, len(weights) // 2),
        grid_spec=pltpu.PrefetchScalarGridSpec(
            num_scalar_prefetch=1,
            grid=(1,),
            in_specs=[pl.BlockSpec(memory_space=pl.ANY)] + [whole] * len(weights),
            out_specs=[whole] * len(weights),
            scratch_shapes=[
                pltpu.VMEM(recv.shape, recv.dtype),
                pltpu.SemaphoreType.DMA((CHUNKS,)),
            ],
        ),
        out_shape=[jax.ShapeDtypeStruct(shape, dtype)] * len(weights),
        compiler_params=pltpu.CompilerParams(vmem_limit_bytes=SLICE_VMEM),
        cost_estimate=pl.CostEstimate(
            flops=8 * recv.shape[0] * w_size,
            bytes_accessed=2 * recv.size + 8 * w_size,
            transcendentals=0,
        ),
        name="slice_grads",
    )(which, recv, *weights)


def moved(block, distance):
    planes = lax.axis_size("x")
    return lax.ppermute(block, "x", [(i, (i + distance) % planes) for i in range(planes)])


def add(*blocks):
    return sum(block.astype(jnp.float32) for block in blocks)


def body(tokens, expert_ids, gate_probs, act_grad, hot_experts, w_gate, w_up):
    width = tokens.shape[1]
    ff = act_grad.shape[2]
    copies = lax.axis_size("yh")
    experts = lax.axis_size(EXPERT)
    planes = lax.axis_size("x")
    here = lax.axis_index("x")
    send = pl.pallas_call(
        pack_kernel,
        out_shape=jax.ShapeDtypeStruct(
            (copies * experts, SLOTS, width + ff // copies), jnp.bfloat16
        ),
        compiler_params=pltpu.CompilerParams(vmem_limit_bytes=VMEM),
        name="pack_rows",
    )(
        expert_ids.T,
        gate_probs.T,
        hot_experts.reshape(1, -1),
        tokens,
        jnp.swapaxes(act_grad, 0, 1),
    )
    send, w_gate, w_up = lax.optimization_barrier((send, w_gate, w_up))
    recv = lax.all_to_all(send, PLANE, 0, 0, tiled=True)
    mine = (w_gate, w_up)
    theirs = {d: tuple(moved(w, -d) for w in mine) for d in (2, 1, 3)}
    at = jnp.stack([(here + d) % planes for d in range(planes)])

    recv, theirs = lax.optimization_barrier((recv.reshape(-1, recv.shape[2]), theirs))
    far_gate, far_up = slice_grads(at[2:3], recv, theirs[2], jnp.bfloat16)
    far_gate_in = moved(far_gate, 1)
    far_up_in = moved(far_up, -1)
    right_gate, right_up, left_gate, left_up = slice_grads(
        at[1::2], recv, theirs[1] + theirs[3], jnp.bfloat16
    )
    from_left_up = moved(right_up, 1)
    from_right_gate = moved(left_gate, -1)
    sum_gate = add(right_gate, far_gate_in).astype(jnp.bfloat16)
    sum_up = add(left_up, far_up_in).astype(jnp.bfloat16)
    from_left_gate = moved(sum_gate, 1)
    from_right_up = moved(sum_up, -1)
    recv, _, _ = lax.optimization_barrier((recv, sum_gate, sum_up))
    own_gate, own_up = slice_grads(at[0:1], recv, mine, jnp.float32)
    grad_gate = add(own_gate, from_right_gate, from_left_gate)
    grad_up = add(own_up, from_left_up, from_right_up)
    return (grad_gate.astype(jnp.bfloat16), grad_up.astype(jnp.bfloat16))


def solution(mesh):
    grid = Mesh(mesh.devices.reshape(2, 4, 4, 8, 2), AXES)
    rows = P(AXES)
    weights = P(EXPERT, None, ("yh", "x"))
    return jax.shard_map(
        body,
        mesh=grid,
        in_specs=(rows, rows, rows, rows, P(), weights, weights),
        out_specs=(weights, weights),
        check_vma=False,
    )
```

```python
import functools

import jax
import jax.numpy as jnp
from jax import lax
from jax.experimental import pallas as pl
from jax.experimental.pallas import tpu as pltpu
from jax.sharding import Mesh, PartitionSpec as P

CAP = 2
OVF = 2
SLOTS = CAP + OVF
VMEM = 60 * 2**20
SLICE_VMEM = 36 * 2**20
AXES = ("yh", "x", "yl", "z", "c")
PLANE = ("yh", "yl", "z", "c")
EXPERT = ("yl", "z", "c")


def pack_kernel(ids_ref, probs_ref, hot_ref, tok_ref, act_ref, out_ref):
    top, block = ids_ref.shape
    experts = out_ref.shape[0] // 2
    rows = experts * SLOTS
    width = tok_ref.shape[1]
    half = out_ref.shape[2] - width
    row = lax.broadcasted_iota(jnp.int32, (rows, block), 0)
    expert, slot = row // SLOTS, row % SLOTS
    hits = [ids_ref[k : k + 1, :] == expert for k in range(top)]
    named = hits[0]
    for hit in hits[1:]:
        named = named | hit
    before = lax.broadcasted_iota(jnp.int32, (block, block), 0) < lax.broadcasted_iota(
        jnp.int32, (block, block), 1
    )
    position = jnp.dot(
        jnp.where(named, 1.0, 0.0).astype(jnp.bfloat16),
        jnp.where(before, 1.0, 0.0).astype(jnp.bfloat16),
        preferred_element_type=jnp.float32,
    ).astype(jnp.int32)
    hots = hot_ref.shape[1]
    owner = lax.broadcasted_iota(jnp.int32, (rows, hots), 0) // SLOTS
    hot = jnp.max(jnp.where(hot_ref[...] == owner, 1, 0), axis=1, keepdims=True)
    kept = named & (position == slot) & ((slot < CAP) | (hot > 0))
    pick = jnp.where(kept, 1.0, 0.0).astype(jnp.bfloat16)
    toks = jnp.dot(pick, tok_ref[...], preferred_element_type=jnp.float32)
    toks = toks.astype(jnp.bfloat16).reshape(experts, SLOTS, width)
    out_ref[:experts, :, :width] = toks
    out_ref[experts:, :, :width] = toks
    acts = jnp.zeros((rows, act_ref.shape[2]), jnp.float32)
    scale = jnp.zeros((rows, block), jnp.float32)
    for k in range(top):
        chosen = jnp.where(kept & hits[k], 1.0, 0.0)
        acts += jnp.dot(chosen.astype(jnp.bfloat16), act_ref[k], preferred_element_type=jnp.float32)
        scale += chosen * probs_ref[k : k + 1, :]
    acts = jnp.sum(scale, axis=1, keepdims=True) * acts
    acts = acts.astype(jnp.bfloat16)
    out_ref[:experts, :, width:] = acts[:, :half].reshape(experts, SLOTS, half)
    out_ref[experts:, :, width:] = acts[:, half:].reshape(experts, SLOTS, half)


def pre_grads(gate, up, act):
    upstream = act.astype(jnp.float32)
    sig = 1.0 / (1.0 + jnp.exp(-gate))
    d_up = upstream * gate * sig
    d_gate = upstream * up * sig * (1.0 + gate * (1.0 - sig))
    return [d_gate.astype(jnp.bfloat16), d_up.astype(jnp.bfloat16)]


CHUNKS = 2
TILES = 5


def slices_kernel(count, which_ref, recv_ref, *refs):
    weights_hbm, grads = refs[: 2 * count], refs[2 * count : 4 * count]
    rows, weights, d, sems = refs[4 * count :]
    width, hidden = weights_hbm[0].shape[1:]
    loads = [
        pltpu.make_async_copy(
            source.at[0], weights.at[j // 2, :, pl.ds(j % 2 * hidden, hidden)], sems.at[j]
        )
        for j, source in enumerate(weights_hbm)
    ]
    for load in loads:
        load.start()
    messages = recv_ref.shape[0] // CHUNKS
    chunk = messages * SLOTS
    for c in range(CHUNKS):
        got = recv_ref[c * messages : (c + 1) * messages]
        rows[c * chunk : (c + 1) * chunk, :] = got.reshape(chunk, rows.shape[1])
    for k in range(count):
        for load in loads[2 * k : 2 * k + 2]:
            load.wait()
        start = pl.multiple_of(width + which_ref[k] * hidden, hidden)
        for c in range(CHUNKS):
            part = slice(c * chunk, (c + 1) * chunk)
            both = jnp.dot(rows[part, :width], weights[k], preferred_element_type=jnp.float32)
            upstream = rows[part, pl.ds(start, hidden)]
            d_gate, d_up = pre_grads(both[:, :hidden], both[:, hidden:], upstream)
            d[part, 2 * k * hidden : (2 * k + 1) * hidden] = d_gate
            d[part, (2 * k + 1) * hidden : (2 * k + 2) * hidden] = d_up
    tile = width // TILES
    for t in range(TILES):
        cols = slice(t * tile, (t + 1) * tile)
        total = lax.dot_general(
            rows[:, cols], d[...], (((0,), (0,)), ((), ())), preferred_element_type=jnp.float32
        )
        for k, ref in enumerate(grads):
            ref[0, cols, :] = total[:, k * hidden : (k + 1) * hidden].astype(ref.dtype)


def slice_grads(which, recv, weights, dtype):
    messages, slots, columns = recv.shape
    shape = weights[0].shape
    _, width, hidden = shape
    count = len(weights) // 2
    rows = messages * slots
    local = pl.BlockSpec(memory_space=pltpu.VMEM)
    anywhere = pl.BlockSpec(memory_space=pl.ANY)
    return pl.pallas_call(
        functools.partial(slices_kernel, count),
        in_specs=[pl.BlockSpec(memory_space=pltpu.SMEM), local] + [anywhere] * len(weights),
        out_specs=[local] * len(weights),
        out_shape=[jax.ShapeDtypeStruct(shape, dtype)] * len(weights),
        scratch_shapes=[
            pltpu.VMEM((rows, columns), recv.dtype),
            pltpu.VMEM((count, width, 2 * hidden), recv.dtype),
            pltpu.VMEM((rows, 2 * count * hidden), recv.dtype),
            pltpu.SemaphoreType.DMA((2 * count,)),
        ],
        compiler_params=pltpu.CompilerParams(vmem_limit_bytes=SLICE_VMEM),
        cost_estimate=pl.CostEstimate(
            flops=8 * rows * count * width * hidden,
            bytes_accessed=2 * recv.size + 8 * count * width * hidden,
            transcendentals=0,
        ),
        name="slice_grads",
    )(which, recv, *weights)


def moved(block, distance):
    planes = lax.axis_size("x")
    return lax.ppermute(block, "x", [(i, (i + distance) % planes) for i in range(planes)])


def add(*blocks):
    return sum(block.astype(jnp.float32) for block in blocks)


def body(tokens, expert_ids, gate_probs, act_grad, hot_experts, w_gate, w_up):
    width = tokens.shape[1]
    ff = act_grad.shape[2]
    copies = lax.axis_size("yh")
    experts = lax.axis_size(EXPERT)
    planes = lax.axis_size("x")
    here = lax.axis_index("x")
    send = pl.pallas_call(
        pack_kernel,
        out_shape=jax.ShapeDtypeStruct(
            (copies * experts, SLOTS, width + ff // copies), jnp.bfloat16
        ),
        compiler_params=pltpu.CompilerParams(vmem_limit_bytes=VMEM),
        name="pack_rows",
    )(
        expert_ids.T,
        gate_probs.T,
        hot_experts.reshape(1, -1),
        tokens,
        jnp.swapaxes(act_grad, 0, 1),
    )
    send, w_gate, w_up = lax.optimization_barrier((send, w_gate, w_up))
    recv = lax.all_to_all(send, PLANE, 0, 0, tiled=True)
    mine = (w_gate, w_up)
    theirs = {d: tuple(moved(w, -d) for w in mine) for d in (2, 1, 3)}
    at = jnp.stack([(here + d) % planes for d in range(planes)])

    recv, theirs = lax.optimization_barrier((recv, theirs))
    far_gate, far_up = slice_grads(at[2:3], recv, theirs[2], jnp.bfloat16)
    far_gate_in = moved(far_gate, 1)
    far_up_in = moved(far_up, -1)
    right_gate, right_up, left_gate, left_up = slice_grads(
        at[1::2], recv, theirs[1] + theirs[3], jnp.bfloat16
    )
    from_left_up = moved(right_up, 1)
    from_right_gate = moved(left_gate, -1)
    sum_gate = add(right_gate, far_gate_in).astype(jnp.bfloat16)
    sum_up = add(left_up, far_up_in).astype(jnp.bfloat16)
    from_left_gate = moved(sum_gate, 1)
    from_right_up = moved(sum_up, -1)
    recv, _, _ = lax.optimization_barrier((recv, sum_gate, sum_up))
    own_gate, own_up = slice_grads(at[0:1], recv, mine, jnp.float32)
    grad_gate = add(own_gate, from_right_gate, from_left_gate)
    grad_up = add(own_up, from_left_up, from_right_up)
    return (grad_gate.astype(jnp.bfloat16), grad_up.astype(jnp.bfloat16))


def solution(mesh):
    grid = Mesh(mesh.devices.reshape(2, 4, 4, 8, 2), AXES)
    rows = P(AXES)
    weights = P(EXPERT, None, ("yh", "x"))
    return jax.shard_map(
        body,
        mesh=grid,
        in_specs=(rows, rows, rows, rows, P(), weights, weights),
        out_specs=(weights, weights),
        check_vma=False,
    )
```

```python
import functools

import jax
import jax.numpy as jnp
from jax import lax
from jax.experimental import pallas as pl
from jax.experimental.pallas import tpu as pltpu
from jax.sharding import Mesh, PartitionSpec as P

CAP = 2
OVF = 2
SLOTS = CAP + OVF
VMEM = 60 * 2**20
SLICE_VMEM = 36 * 2**20
AXES = ("yh", "x", "yl", "z", "c")
PLANE = ("yh", "yl", "z", "c")
EXPERT = ("yl", "z", "c")


def pack_kernel(ids_ref, probs_ref, hot_ref, tok_ref, act_ref, out_ref):
    top, block = ids_ref.shape
    experts = out_ref.shape[0] // 2
    rows = experts * SLOTS
    width = tok_ref.shape[1]
    half = out_ref.shape[2] - width
    row = lax.broadcasted_iota(jnp.int32, (rows, block), 0)
    expert, slot = row // SLOTS, row % SLOTS
    hits = [ids_ref[k : k + 1, :] == expert for k in range(top)]
    named = hits[0]
    for hit in hits[1:]:
        named = named | hit
    before = lax.broadcasted_iota(jnp.int32, (block, block), 0) < lax.broadcasted_iota(
        jnp.int32, (block, block), 1
    )
    position = jnp.dot(
        jnp.where(named, 1.0, 0.0).astype(jnp.bfloat16),
        jnp.where(before, 1.0, 0.0).astype(jnp.bfloat16),
        preferred_element_type=jnp.float32,
    ).astype(jnp.int32)
    hots = hot_ref.shape[1]
    owner = lax.broadcasted_iota(jnp.int32, (rows, hots), 0) // SLOTS
    hot = jnp.max(jnp.where(hot_ref[...] == owner, 1, 0), axis=1, keepdims=True)
    kept = named & (position == slot) & ((slot < CAP) | (hot > 0))
    pick = jnp.where(kept, 1.0, 0.0).astype(jnp.bfloat16)
    toks = jnp.dot(pick, tok_ref[...], preferred_element_type=jnp.float32)
    toks = toks.astype(jnp.bfloat16).reshape(experts, SLOTS, width)
    out_ref[:experts, :, :width] = toks
    out_ref[experts:, :, :width] = toks
    acts = jnp.zeros((rows, act_ref.shape[2]), jnp.float32)
    scale = jnp.zeros((rows, block), jnp.float32)
    for k in range(top):
        chosen = jnp.where(kept & hits[k], 1.0, 0.0)
        acts += jnp.dot(chosen.astype(jnp.bfloat16), act_ref[k], preferred_element_type=jnp.float32)
        scale += chosen * probs_ref[k : k + 1, :]
    acts = jnp.sum(scale, axis=1, keepdims=True) * acts
    acts = acts.astype(jnp.bfloat16)
    out_ref[:experts, :, width:] = acts[:, :half].reshape(experts, SLOTS, half)
    out_ref[experts:, :, width:] = acts[:, half:].reshape(experts, SLOTS, half)


def pre_grads(gate, up, act):
    upstream = act.astype(jnp.float32)
    sig = 1.0 / (1.0 + jnp.exp(-gate))
    d_up = upstream * gate * sig
    d_gate = upstream * up * sig * (1.0 + gate * (1.0 - sig))
    return [d_gate.astype(jnp.bfloat16), d_up.astype(jnp.bfloat16)]


CHUNKS = 2
TILES = 5


def slices_kernel(count, which_ref, recv_ref, *refs):
    weights_hbm, grads = refs[: 2 * count], refs[2 * count : 4 * count]
    rows, weights, d, sems = refs[4 * count :]
    width, hidden = weights_hbm[0].shape[1:]
    loads = [
        pltpu.make_async_copy(
            source.at[0], weights.at[j // 2, :, pl.ds(j % 2 * hidden, hidden)], sems.at[j]
        )
        for j, source in enumerate(weights_hbm)
    ]
    for load in loads:
        load.start()
    messages = recv_ref.shape[0] // CHUNKS
    chunk = messages * SLOTS
    for c in range(CHUNKS):
        got = recv_ref[c * messages : (c + 1) * messages]
        rows[c * chunk : (c + 1) * chunk, :] = got.reshape(chunk, rows.shape[1])
    for k in range(count):
        for load in loads[2 * k : 2 * k + 2]:
            load.wait()
        start = pl.multiple_of(width + which_ref[k] * hidden, hidden)
        for c in range(CHUNKS):
            part = slice(c * chunk, (c + 1) * chunk)
            both = jnp.dot(rows[part, :width], weights[k], preferred_element_type=jnp.float32)
            upstream = rows[part, pl.ds(start, hidden)]
            d_gate, d_up = pre_grads(both[:, :hidden], both[:, hidden:], upstream)
            d[part, 2 * k * hidden : (2 * k + 1) * hidden] = d_gate
            d[part, (2 * k + 1) * hidden : (2 * k + 2) * hidden] = d_up
    tile = width // TILES
    for t in range(TILES):
        cols = slice(t * tile, (t + 1) * tile)
        total = lax.dot_general(
            rows[:, cols], d[...], (((0,), (0,)), ((), ())), preferred_element_type=jnp.float32
        )
        for k, ref in enumerate(grads):
            ref[0, cols, :] = total[:, k * hidden : (k + 1) * hidden].astype(ref.dtype)


def slice_grads(which, recv, weights, dtype):
    messages, slots, columns = recv.shape
    shape = weights[0].shape
    _, width, hidden = shape
    count = len(weights) // 2
    rows = messages * slots
    local = pl.BlockSpec(memory_space=pltpu.VMEM)
    anywhere = pl.BlockSpec(memory_space=pl.ANY)
    return pl.pallas_call(
        functools.partial(slices_kernel, count),
        in_specs=[pl.BlockSpec(memory_space=pltpu.SMEM), local] + [anywhere] * len(weights),
        out_specs=[local] * len(weights),
        out_shape=[jax.ShapeDtypeStruct(shape, dtype)] * len(weights),
        scratch_shapes=[
            pltpu.VMEM((rows, columns), recv.dtype),
            pltpu.VMEM((count, width, 2 * hidden), recv.dtype),
            pltpu.VMEM((rows, 2 * count * hidden), recv.dtype),
            pltpu.SemaphoreType.DMA((2 * count,)),
        ],
        compiler_params=pltpu.CompilerParams(vmem_limit_bytes=SLICE_VMEM),
        cost_estimate=pl.CostEstimate(
            flops=8 * rows * count * width * hidden,
            bytes_accessed=2 * recv.size + 8 * count * width * hidden,
            transcendentals=0,
        ),
        name="slice_grads",
    )(which, recv, *weights)


def last_kernel(*refs):
    for ref, terms in ((refs[6], refs[:3]), (refs[7], refs[3:6])):
        ref[...] = sum(term[...].astype(jnp.float32) for term in terms).astype(ref.dtype)


def last_sums(*terms):
    shape = jax.ShapeDtypeStruct(terms[0].shape, jnp.bfloat16)
    return pl.pallas_call(
        last_kernel,
        out_shape=[shape] * 2,
        compiler_params=pltpu.CompilerParams(vmem_limit_bytes=SLICE_VMEM),
        cost_estimate=pl.CostEstimate(
            flops=4 * terms[0].size, bytes_accessed=20 * terms[0].size, transcendentals=0
        ),
        name="last_sums",
    )(*terms)


def moved(block, distance):
    planes = lax.axis_size("x")
    return lax.ppermute(block, "x", [(i, (i + distance) % planes) for i in range(planes)])


def add(*blocks):
    return sum(block.astype(jnp.float32) for block in blocks)


def body(tokens, expert_ids, gate_probs, act_grad, hot_experts, w_gate, w_up):
    width = tokens.shape[1]
    ff = act_grad.shape[2]
    copies = lax.axis_size("yh")
    experts = lax.axis_size(EXPERT)
    planes = lax.axis_size("x")
    here = lax.axis_index("x")
    send = pl.pallas_call(
        pack_kernel,
        out_shape=jax.ShapeDtypeStruct(
            (copies * experts, SLOTS, width + ff // copies), jnp.bfloat16
        ),
        compiler_params=pltpu.CompilerParams(vmem_limit_bytes=VMEM),
        name="pack_rows",
    )(
        expert_ids.T,
        gate_probs.T,
        hot_experts.reshape(1, -1),
        tokens,
        jnp.swapaxes(act_grad, 0, 1),
    )
    send, w_gate, w_up = lax.optimization_barrier((send, w_gate, w_up))
    recv = lax.all_to_all(send, PLANE, 0, 0, tiled=True)
    mine = (w_gate, w_up)
    theirs = {d: tuple(moved(w, -d) for w in mine) for d in (2, 1, 3)}
    at = jnp.stack([(here + d) % planes for d in (0, 2, 1, 3)])

    recv, theirs = lax.optimization_barrier((recv, theirs))
    far_gate, far_up, right_gate, right_up, left_gate, left_up = slice_grads(
        at[1:], recv, theirs[2] + theirs[1] + theirs[3], jnp.bfloat16
    )
    far_gate_in = moved(far_gate, 1)
    far_up_in = moved(far_up, -1)
    from_left_up = moved(right_up, 1)
    from_right_gate = moved(left_gate, -1)
    sum_gate = add(right_gate, far_gate_in).astype(jnp.bfloat16)
    sum_up = add(left_up, far_up_in).astype(jnp.bfloat16)
    from_left_gate = moved(sum_gate, 1)
    from_right_up = moved(sum_up, -1)
    recv, _, _ = lax.optimization_barrier((recv, sum_gate, sum_up))
    own_gate, own_up = slice_grads(at[0:1], recv, mine, jnp.float32)
    return last_sums(
        own_gate, from_right_gate, from_left_gate, own_up, from_left_up, from_right_up
    )


def solution(mesh):
    grid = Mesh(mesh.devices.reshape(2, 4, 4, 8, 2), AXES)
    rows = P(AXES)
    weights = P(EXPERT, None, ("yh", "x"))
    return jax.shard_map(
        body,
        mesh=grid,
        in_specs=(rows, rows, rows, rows, P(), weights, weights),
        out_specs=(weights, weights),
        check_vma=False,
    )
```

```python
import functools

import jax
import jax.numpy as jnp
from jax import lax
from jax.experimental import pallas as pl
from jax.experimental.pallas import tpu as pltpu
from jax.sharding import Mesh, PartitionSpec as P

CAP = 2
OVF = 2
SLOTS = CAP + OVF
VMEM = 60 * 2**20
SLICE_VMEM = 36 * 2**20
AXES = ("yh", "x", "yl", "z", "c")
PLANE = ("yh", "yl", "z", "c")
EXPERT = ("yl", "z", "c")


def pack_kernel(ids_ref, probs_ref, hot_ref, tok_ref, act_ref, out_ref):
    top, block = ids_ref.shape
    experts = out_ref.shape[0] // 2
    rows = experts * SLOTS
    width = tok_ref.shape[1]
    half = out_ref.shape[2] - width
    row = lax.broadcasted_iota(jnp.int32, (rows, block), 0)
    expert, slot = row // SLOTS, row % SLOTS
    hits = [ids_ref[k : k + 1, :] == expert for k in range(top)]
    named = hits[0]
    for hit in hits[1:]:
        named = named | hit
    before = lax.broadcasted_iota(jnp.int32, (block, block), 0) < lax.broadcasted_iota(
        jnp.int32, (block, block), 1
    )
    position = jnp.dot(
        jnp.where(named, 1.0, 0.0).astype(jnp.bfloat16),
        jnp.where(before, 1.0, 0.0).astype(jnp.bfloat16),
        preferred_element_type=jnp.float32,
    ).astype(jnp.int32)
    hots = hot_ref.shape[1]
    owner = lax.broadcasted_iota(jnp.int32, (rows, hots), 0) // SLOTS
    hot = jnp.max(jnp.where(hot_ref[...] == owner, 1, 0), axis=1, keepdims=True)
    kept = named & (position == slot) & ((slot < CAP) | (hot > 0))
    pick = jnp.where(kept, 1.0, 0.0).astype(jnp.bfloat16)
    toks = jnp.dot(pick, tok_ref[...], preferred_element_type=jnp.float32)
    toks = toks.astype(jnp.bfloat16).reshape(experts, SLOTS, width)
    out_ref[:experts, :, :width] = toks
    out_ref[experts:, :, :width] = toks
    acts = jnp.zeros((rows, act_ref.shape[2]), jnp.float32)
    scale = jnp.zeros((rows, block), jnp.float32)
    for k in range(top):
        chosen = jnp.where(kept & hits[k], 1.0, 0.0)
        acts += jnp.dot(chosen.astype(jnp.bfloat16), act_ref[k], preferred_element_type=jnp.float32)
        scale += chosen * probs_ref[k : k + 1, :]
    acts = jnp.sum(scale, axis=1, keepdims=True) * acts
    acts = acts.astype(jnp.bfloat16)
    out_ref[:experts, :, width:] = acts[:, :half].reshape(experts, SLOTS, half)
    out_ref[experts:, :, width:] = acts[:, half:].reshape(experts, SLOTS, half)


def pre_grads(gate, up, act):
    upstream = act.astype(jnp.float32)
    sig = 1.0 / (1.0 + jnp.exp(-gate))
    d_up = upstream * gate * sig
    d_gate = upstream * up * sig * (1.0 + gate * (1.0 - sig))
    return [d_gate.astype(jnp.bfloat16), d_up.astype(jnp.bfloat16)]


CHUNKS = 2
TILES = 5


def slices_kernel(count, which_ref, recv_ref, *refs):
    weights_hbm, grads = refs[: 2 * count], refs[2 * count : 4 * count]
    rows, weights, d, sems = refs[4 * count :]
    width, hidden = weights_hbm[0].shape[1:]
    loads = [
        pltpu.make_async_copy(
            source.at[0], weights.at[j // 2, :, pl.ds(j % 2 * hidden, hidden)], sems.at[j]
        )
        for j, source in enumerate(weights_hbm)
    ]
    for load in loads:
        load.start()
    messages = recv_ref.shape[0] // CHUNKS
    chunk = messages * SLOTS
    for c in range(CHUNKS):
        got = recv_ref[c * messages : (c + 1) * messages]
        rows[c * chunk : (c + 1) * chunk, :] = got.reshape(chunk, rows.shape[1])
    for k in range(count):
        for load in loads[2 * k : 2 * k + 2]:
            load.wait()
        start = pl.multiple_of(width + which_ref[k] * hidden, hidden)
        for c in range(CHUNKS):
            part = slice(c * chunk, (c + 1) * chunk)
            both = jnp.dot(rows[part, :width], weights[k], preferred_element_type=jnp.float32)
            upstream = rows[part, pl.ds(start, hidden)]
            d_gate, d_up = pre_grads(both[:, :hidden], both[:, hidden:], upstream)
            d[part, 2 * k * hidden : (2 * k + 1) * hidden] = d_gate
            d[part, (2 * k + 1) * hidden : (2 * k + 2) * hidden] = d_up
    tile = width // TILES
    for t in range(TILES):
        cols = slice(t * tile, (t + 1) * tile)
        total = lax.dot_general(
            rows[:, cols], d[...], (((0,), (0,)), ((), ())), preferred_element_type=jnp.float32
        )
        for k, ref in enumerate(grads):
            ref[0, cols, :] = total[:, k * hidden : (k + 1) * hidden].astype(ref.dtype)


def slice_grads(which, recv, weights, dtype):
    messages, slots, columns = recv.shape
    shape = weights[0].shape
    _, width, hidden = shape
    count = len(weights) // 2
    rows = messages * slots
    local = pl.BlockSpec(memory_space=pltpu.VMEM)
    anywhere = pl.BlockSpec(memory_space=pl.ANY)
    return pl.pallas_call(
        functools.partial(slices_kernel, count),
        in_specs=[pl.BlockSpec(memory_space=pltpu.SMEM), local] + [anywhere] * len(weights),
        out_specs=[local] * len(weights),
        out_shape=[jax.ShapeDtypeStruct(shape, dtype)] * len(weights),
        scratch_shapes=[
            pltpu.VMEM((rows, columns), recv.dtype),
            pltpu.VMEM((count, width, 2 * hidden), recv.dtype),
            pltpu.VMEM((rows, 2 * count * hidden), recv.dtype),
            pltpu.SemaphoreType.DMA((2 * count,)),
        ],
        compiler_params=pltpu.CompilerParams(vmem_limit_bytes=SLICE_VMEM),
        cost_estimate=pl.CostEstimate(
            flops=8 * rows * count * width * hidden,
            bytes_accessed=2 * recv.size + 8 * count * width * hidden,
            transcendentals=0,
        ),
        name="slice_grads",
    )(which, recv, *weights)


def moved(block, distance):
    planes = lax.axis_size("x")
    return lax.ppermute(block, "x", [(i, (i + distance) % planes) for i in range(planes)])


def add(*blocks):
    return sum(block.astype(jnp.float32) for block in blocks)


def body(tokens, expert_ids, gate_probs, act_grad, hot_experts, w_gate, w_up):
    width = tokens.shape[1]
    ff = act_grad.shape[2]
    copies = lax.axis_size("yh")
    experts = lax.axis_size(EXPERT)
    planes = lax.axis_size("x")
    here = lax.axis_index("x")
    send = pl.pallas_call(
        pack_kernel,
        out_shape=jax.ShapeDtypeStruct(
            (copies * experts, SLOTS, width + ff // copies), jnp.bfloat16
        ),
        compiler_params=pltpu.CompilerParams(vmem_limit_bytes=VMEM),
        name="pack_rows",
    )(
        expert_ids.T,
        gate_probs.T,
        hot_experts.reshape(1, -1),
        tokens,
        jnp.swapaxes(act_grad, 0, 1),
    )
    send, w_gate, w_up = lax.optimization_barrier((send, w_gate, w_up))
    recv = lax.all_to_all(send, PLANE, 0, 0, tiled=True)
    mine = (w_gate, w_up)
    theirs = {d: tuple(moved(w, -d) for w in mine) for d in (2, 1, 3)}
    at = jnp.stack([(here + d) % planes for d in range(planes)])

    recv, theirs = lax.optimization_barrier((recv, theirs))
    far_gate, far_up = slice_grads(at[2:3], recv, theirs[2], jnp.bfloat16)
    far_gate_in = moved(far_gate, 1)
    far_up_in = moved(far_up, -1)
    right_gate, right_up, left_gate, left_up = slice_grads(
        at[1::2], recv, theirs[1] + theirs[3], jnp.bfloat16
    )
    from_left_up = moved(right_up, 1)
    from_right_gate = moved(left_gate, -1)
    sum_gate = add(right_gate, far_gate_in).astype(jnp.bfloat16)
    from_left_gate = moved(sum_gate, 1)
    sum_up = add(left_up, far_up_in).astype(jnp.bfloat16)
    from_right_up = moved(sum_up, -1)
    recv, _, _ = lax.optimization_barrier((recv, sum_gate, sum_up))
    own_gate, own_up = slice_grads(at[0:1], recv, mine, jnp.float32)
    own_gate, own_up, from_left_up, from_right_gate = lax.optimization_barrier(
        (own_gate, own_up, from_left_up, from_right_gate)
    )
    grad_gate = add(own_gate, from_right_gate, from_left_gate)
    grad_up = add(own_up, from_left_up, from_right_up)
    return (grad_gate.astype(jnp.bfloat16), grad_up.astype(jnp.bfloat16))


def solution(mesh):
    grid = Mesh(mesh.devices.reshape(2, 4, 4, 8, 2), AXES)
    rows = P(AXES)
    weights = P(EXPERT, None, ("yh", "x"))
    return jax.shard_map(
        body,
        mesh=grid,
        in_specs=(rows, rows, rows, rows, P(), weights, weights),
        out_specs=(weights, weights),
        check_vma=False,
    )
```

```python
import functools

import jax
import jax.numpy as jnp
from jax import lax
from jax.experimental import pallas as pl
from jax.experimental.pallas import tpu as pltpu
from jax.sharding import Mesh, PartitionSpec as P

CAP = 2
PIECES = 2
OVF = 2
SLOTS = CAP + OVF
VMEM = 60 * 2**20
SLICE_VMEM = 36 * 2**20
AXES = ("yh", "x", "yl", "z", "c")
PLANE = ("yh", "yl", "z", "c")
EXPERT = ("yl", "z", "c")


def pack_kernel(ids_hbm, hot_hbm, tok_hbm, act_hbm, probs_hbm, out_hbm, *scratch):
    ids_ref, hot_ref, tok_ref, act_ref, probs_ref, toks, acts, in_sems, out_sems = scratch
    top, block = ids_ref.shape
    experts = toks.shape[0]
    rows = experts * SLOTS
    width = tok_ref.shape[1]
    half = acts.shape[2]
    pairs = [(ids_hbm, ids_ref), (hot_hbm, hot_ref), (tok_hbm, tok_ref), (probs_hbm, probs_ref)]
    pairs += [(act_hbm.at[k], act_ref.at[k]) for k in range(top)]
    loads = [pltpu.make_async_copy(*pair, in_sems.at[i]) for i, pair in enumerate(pairs)]
    for load in loads:
        load.start()
    loads[0].wait()
    row = lax.broadcasted_iota(jnp.int32, (rows, block), 0)
    expert, slot = row // SLOTS, row % SLOTS
    hits = [ids_ref[k : k + 1, :] == expert for k in range(top)]
    named = hits[0]
    for hit in hits[1:]:
        named = named | hit
    before = lax.broadcasted_iota(jnp.int32, (block, block), 0) < lax.broadcasted_iota(
        jnp.int32, (block, block), 1
    )
    position = jnp.dot(
        jnp.where(named, 1.0, 0.0).astype(jnp.bfloat16),
        jnp.where(before, 1.0, 0.0).astype(jnp.bfloat16),
        preferred_element_type=jnp.float32,
    ).astype(jnp.int32)
    loads[1].wait()
    hots = hot_ref.shape[1]
    owner = lax.broadcasted_iota(jnp.int32, (rows, hots), 0) // SLOTS
    hot = jnp.max(jnp.where(hot_ref[...] == owner, 1, 0), axis=1, keepdims=True)
    kept = named & (position == slot) & ((slot < CAP) | (hot > 0))
    pick = jnp.where(kept, 1.0, 0.0).astype(jnp.bfloat16)
    sends = []
    loads[2].wait()
    piece = width // PIECES
    for p in range(PIECES):
        cols = slice(p * piece, (p + 1) * piece)
        got = jnp.dot(pick, tok_ref[:, cols], preferred_element_type=jnp.float32)
        toks[:, :, cols] = got.astype(jnp.bfloat16).reshape(experts, SLOTS, piece)
        for copy in range(2):
            part = (pl.ds(copy * experts, experts), slice(None), pl.ds(p * piece, piece))
            sends.append(
                pltpu.make_async_copy(
                    toks.at[:, :, pl.ds(p * piece, piece)], out_hbm.at[part], out_sems.at[p, copy]
                )
            )
            sends[-1].start()
    total = jnp.zeros((rows, act_ref.shape[2]), jnp.float32)
    scale = jnp.zeros((rows, block), jnp.float32)
    loads[3].wait()
    for k in range(top):
        loads[4 + k].wait()
        chosen = jnp.where(kept & hits[k], 1.0, 0.0)
        total += jnp.dot(chosen.astype(jnp.bfloat16), act_ref[k], preferred_element_type=jnp.float32)
        scale += chosen * probs_ref[k : k + 1, :]
    total = (jnp.sum(scale, axis=1, keepdims=True) * total).astype(jnp.bfloat16)
    for copy in range(2):
        here = slice(copy * experts, (copy + 1) * experts)
        acts[here] = total[:, copy * half : (copy + 1) * half].reshape(experts, SLOTS, half)
    sends.append(
        pltpu.make_async_copy(acts, out_hbm.at[:, :, pl.ds(width, half)], out_sems.at[PIECES, 0])
    )
    sends[-1].start()
    for send in sends:
        send.wait()


def pre_grads(gate, up, act):
    upstream = act.astype(jnp.float32)
    sig = 1.0 / (1.0 + jnp.exp(-gate))
    d_up = upstream * gate * sig
    d_gate = upstream * up * sig * (1.0 + gate * (1.0 - sig))
    return [d_gate.astype(jnp.bfloat16), d_up.astype(jnp.bfloat16)]


CHUNKS = 2
TILES = 5


def slices_kernel(count, which_ref, recv_ref, *refs):
    weights_hbm, grads = refs[: 2 * count], refs[2 * count : 4 * count]
    rows, weights, d, sems = refs[4 * count :]
    width, hidden = weights_hbm[0].shape[1:]
    loads = [
        pltpu.make_async_copy(
            source.at[0], weights.at[j // 2, :, pl.ds(j % 2 * hidden, hidden)], sems.at[j]
        )
        for j, source in enumerate(weights_hbm)
    ]
    for load in loads:
        load.start()
    messages = recv_ref.shape[0] // CHUNKS
    chunk = messages * SLOTS
    for c in range(CHUNKS):
        got = recv_ref[c * messages : (c + 1) * messages]
        rows[c * chunk : (c + 1) * chunk, :] = got.reshape(chunk, rows.shape[1])
    for k in range(count):
        for load in loads[2 * k : 2 * k + 2]:
            load.wait()
        start = pl.multiple_of(width + which_ref[k] * hidden, hidden)
        for c in range(CHUNKS):
            part = slice(c * chunk, (c + 1) * chunk)
            both = jnp.dot(rows[part, :width], weights[k], preferred_element_type=jnp.float32)
            upstream = rows[part, pl.ds(start, hidden)]
            d_gate, d_up = pre_grads(both[:, :hidden], both[:, hidden:], upstream)
            d[part, 2 * k * hidden : (2 * k + 1) * hidden] = d_gate
            d[part, (2 * k + 1) * hidden : (2 * k + 2) * hidden] = d_up
    tile = width // TILES
    for t in range(TILES):
        cols = slice(t * tile, (t + 1) * tile)
        total = lax.dot_general(
            rows[:, cols], d[...], (((0,), (0,)), ((), ())), preferred_element_type=jnp.float32
        )
        for k, ref in enumerate(grads):
            ref[0, cols, :] = total[:, k * hidden : (k + 1) * hidden].astype(ref.dtype)


def slice_grads(which, recv, weights, dtype):
    messages, slots, columns = recv.shape
    shape = weights[0].shape
    _, width, hidden = shape
    count = len(weights) // 2
    rows = messages * slots
    local = pl.BlockSpec(memory_space=pltpu.VMEM)
    anywhere = pl.BlockSpec(memory_space=pl.ANY)
    return pl.pallas_call(
        functools.partial(slices_kernel, count),
        in_specs=[pl.BlockSpec(memory_space=pltpu.SMEM), local] + [anywhere] * len(weights),
        out_specs=[local] * len(weights),
        out_shape=[jax.ShapeDtypeStruct(shape, dtype)] * len(weights),
        scratch_shapes=[
            pltpu.VMEM((rows, columns), recv.dtype),
            pltpu.VMEM((count, width, 2 * hidden), recv.dtype),
            pltpu.VMEM((rows, 2 * count * hidden), recv.dtype),
            pltpu.SemaphoreType.DMA((2 * count,)),
        ],
        compiler_params=pltpu.CompilerParams(vmem_limit_bytes=SLICE_VMEM),
        cost_estimate=pl.CostEstimate(
            flops=8 * rows * count * width * hidden,
            bytes_accessed=2 * recv.size + 8 * count * width * hidden,
            transcendentals=0,
        ),
        name="slice_grads",
    )(which, recv, *weights)


def moved(block, distance):
    planes = lax.axis_size("x")
    return lax.ppermute(block, "x", [(i, (i + distance) % planes) for i in range(planes)])


def add(*blocks):
    return sum(block.astype(jnp.float32) for block in blocks)


def body(tokens, expert_ids, gate_probs, act_grad, hot_experts, w_gate, w_up):
    width = tokens.shape[1]
    ff = act_grad.shape[2]
    copies = lax.axis_size("yh")
    experts = lax.axis_size(EXPERT)
    planes = lax.axis_size("x")
    here = lax.axis_index("x")
    anywhere = pl.BlockSpec(memory_space=pl.ANY)
    block, top, _ = act_grad.shape
    vmem = lambda *shape: pltpu.VMEM(shape, jnp.bfloat16)
    send = pl.pallas_call(
        pack_kernel,
        in_specs=[anywhere] * 5,
        out_specs=anywhere,
        out_shape=jax.ShapeDtypeStruct(
            (copies * experts, SLOTS, width + ff // copies), jnp.bfloat16
        ),
        scratch_shapes=[
            pltpu.VMEM((top, block), jnp.int32),
            pltpu.VMEM((1, hot_experts.size), jnp.int32),
            vmem(block, width),
            vmem(top, block, ff),
            pltpu.VMEM((top, block), jnp.float32),
            vmem(experts, SLOTS, width),
            vmem(copies * experts, SLOTS, ff // copies),
            pltpu.SemaphoreType.DMA((4 + top,)),
            pltpu.SemaphoreType.DMA((PIECES + 1, copies)),
        ],
        compiler_params=pltpu.CompilerParams(vmem_limit_bytes=VMEM),
        name="pack_rows",
    )(
        expert_ids.T,
        hot_experts.reshape(1, -1),
        tokens,
        jnp.swapaxes(act_grad, 0, 1),
        gate_probs.T,
    )
    send, w_gate, w_up = lax.optimization_barrier((send, w_gate, w_up))
    recv = lax.all_to_all(send, PLANE, 0, 0, tiled=True)
    mine = (w_gate, w_up)
    theirs = {d: tuple(moved(w, -d) for w in mine) for d in (2, 1, 3)}
    at = jnp.stack([(here + d) % planes for d in range(planes)])

    recv, theirs = lax.optimization_barrier((recv, theirs))
    far_gate, far_up = slice_grads(at[2:3], recv, theirs[2], jnp.bfloat16)
    far_gate_in = moved(far_gate, 1)
    far_up_in = moved(far_up, -1)
    right_gate, right_up, left_gate, left_up = slice_grads(
        at[1::2], recv, theirs[1] + theirs[3], jnp.bfloat16
    )
    from_left_up = moved(right_up, 1)
    from_right_gate = moved(left_gate, -1)
    sum_gate = add(right_gate, far_gate_in).astype(jnp.bfloat16)
    from_left_gate = moved(sum_gate, 1)
    sum_up = add(left_up, far_up_in).astype(jnp.bfloat16)
    from_right_up = moved(sum_up, -1)
    recv, _, _ = lax.optimization_barrier((recv, sum_gate, sum_up))
    own_gate, own_up = slice_grads(at[0:1], recv, mine, jnp.float32)
    own_gate, own_up, from_left_up, from_right_gate = lax.optimization_barrier(
        (own_gate, own_up, from_left_up, from_right_gate)
    )
    grad_gate = add(own_gate, from_right_gate, from_left_gate)
    grad_up = add(own_up, from_left_up, from_right_up)
    return (grad_gate.astype(jnp.bfloat16), grad_up.astype(jnp.bfloat16))


def solution(mesh):
    grid = Mesh(mesh.devices.reshape(2, 4, 4, 8, 2), AXES)
    rows = P(AXES)
    weights = P(EXPERT, None, ("yh", "x"))
    return jax.shard_map(
        body,
        mesh=grid,
        in_specs=(rows, rows, rows, rows, P(), weights, weights),
        out_specs=(weights, weights),
        check_vma=False,
    )
```

```python
import functools

import jax
import jax.numpy as jnp
from jax import lax
from jax.experimental import pallas as pl
from jax.experimental.pallas import tpu as pltpu
from jax.sharding import Mesh, PartitionSpec as P

CAP = 2
PIECES = 2
OVF = 2
SLOTS = CAP + OVF
VMEM = 60 * 2**20
SLICE_VMEM = 36 * 2**20
AXES = ("yh", "x", "yl", "z", "c")
PLANE = ("yh", "yl", "z", "c")
EXPERT = ("yl", "z", "c")


def pack_kernel(ids_hbm, hot_hbm, tok_hbm, act_hbm, probs_hbm, out_hbm, *scratch):
    ids_ref, hot_ref, tok_ref, act_ref, probs_ref, toks, acts, in_sems, out_sems = scratch
    top, block = ids_ref.shape
    experts = toks.shape[0]
    rows = experts * SLOTS
    width = tok_ref.shape[1]
    half = acts.shape[2]
    pairs = [(ids_hbm, ids_ref), (hot_hbm, hot_ref), (tok_hbm, tok_ref), (probs_hbm, probs_ref)]
    pairs += [(act_hbm.at[k], act_ref.at[k]) for k in range(top)]
    loads = [pltpu.make_async_copy(*pair, in_sems.at[i]) for i, pair in enumerate(pairs)]
    for load in loads:
        load.start()
    loads[0].wait()
    row = lax.broadcasted_iota(jnp.int32, (rows, block), 0)
    expert, slot = row // SLOTS, row % SLOTS
    hits = [ids_ref[k : k + 1, :] == expert for k in range(top)]
    named = hits[0]
    for hit in hits[1:]:
        named = named | hit
    before = lax.broadcasted_iota(jnp.int32, (block, block), 0) < lax.broadcasted_iota(
        jnp.int32, (block, block), 1
    )
    position = jnp.dot(
        jnp.where(named, 1.0, 0.0).astype(jnp.bfloat16),
        jnp.where(before, 1.0, 0.0).astype(jnp.bfloat16),
        preferred_element_type=jnp.float32,
    ).astype(jnp.int32)
    loads[1].wait()
    hots = hot_ref.shape[1]
    owner = lax.broadcasted_iota(jnp.int32, (rows, hots), 0) // SLOTS
    hot = jnp.max(jnp.where(hot_ref[...] == owner, 1, 0), axis=1, keepdims=True)
    kept = named & (position == slot) & ((slot < CAP) | (hot > 0))
    pick = jnp.where(kept, 1.0, 0.0).astype(jnp.bfloat16)
    sends = []
    loads[2].wait()
    piece = width // PIECES
    for p in range(PIECES):
        cols = slice(p * piece, (p + 1) * piece)
        got = jnp.dot(pick, tok_ref[:, cols], preferred_element_type=jnp.float32)
        toks[:, :, cols] = got.astype(jnp.bfloat16).reshape(experts, SLOTS, piece)
        for copy in range(2):
            part = (pl.ds(copy * experts, experts), slice(None), pl.ds(p * piece, piece))
            sends.append(
                pltpu.make_async_copy(
                    toks.at[:, :, pl.ds(p * piece, piece)], out_hbm.at[part], out_sems.at[p, copy]
                )
            )
            sends[-1].start()
    total = jnp.zeros((rows, act_ref.shape[2]), jnp.float32)
    scale = jnp.zeros((rows, block), jnp.float32)
    loads[3].wait()
    for k in range(top):
        loads[4 + k].wait()
        chosen = jnp.where(kept & hits[k], 1.0, 0.0)
        total += jnp.dot(chosen.astype(jnp.bfloat16), act_ref[k], preferred_element_type=jnp.float32)
        scale += chosen * probs_ref[k : k + 1, :]
    total = (jnp.sum(scale, axis=1, keepdims=True) * total).astype(jnp.bfloat16)
    for copy in range(2):
        here = slice(copy * experts, (copy + 1) * experts)
        acts[here] = total[:, copy * half : (copy + 1) * half].reshape(experts, SLOTS, half)
    sends.append(
        pltpu.make_async_copy(acts, out_hbm.at[:, :, pl.ds(width, half)], out_sems.at[PIECES, 0])
    )
    sends[-1].start()
    for send in sends:
        send.wait()


def pre_grads(gate, up, act):
    upstream = act.astype(jnp.float32)
    sig = 1.0 / (1.0 + jnp.exp(-gate))
    d_up = upstream * gate * sig
    d_gate = upstream * up * sig * (1.0 + gate * (1.0 - sig))
    return [d_gate.astype(jnp.bfloat16), d_up.astype(jnp.bfloat16)]


CHUNKS = 2
TILES = 5


def slices_kernel(count, which_ref, recv_ref, *refs):
    weights_hbm, grads = refs[: 2 * count], refs[2 * count : 4 * count]
    rows, weights, d, sems = refs[4 * count :]
    width, hidden = weights_hbm[0].shape[1:]
    loads = [
        pltpu.make_async_copy(
            source.at[0], weights.at[j // 2, :, pl.ds(j % 2 * hidden, hidden)], sems.at[j]
        )
        for j, source in enumerate(weights_hbm)
    ]
    for load in loads:
        load.start()
    messages = recv_ref.shape[0] // CHUNKS
    chunk = messages * SLOTS
    for c in range(CHUNKS):
        got = recv_ref[c * messages : (c + 1) * messages]
        rows[c * chunk : (c + 1) * chunk, :] = got.reshape(chunk, rows.shape[1])
    for k in range(count):
        for load in loads[2 * k : 2 * k + 2]:
            load.wait()
        start = pl.multiple_of(width + which_ref[k] * hidden, hidden)
        for c in range(CHUNKS):
            part = slice(c * chunk, (c + 1) * chunk)
            both = jnp.dot(rows[part, :width], weights[k], preferred_element_type=jnp.float32)
            upstream = rows[part, pl.ds(start, hidden)]
            d_gate, d_up = pre_grads(both[:, :hidden], both[:, hidden:], upstream)
            d[part, 2 * k * hidden : (2 * k + 1) * hidden] = d_gate
            d[part, (2 * k + 1) * hidden : (2 * k + 2) * hidden] = d_up
    tile = width // TILES
    for t in range(TILES):
        cols = slice(t * tile, (t + 1) * tile)
        total = lax.dot_general(
            rows[:, cols], d[...], (((0,), (0,)), ((), ())), preferred_element_type=jnp.float32
        )
        for k, ref in enumerate(grads):
            ref[0, cols, :] = total[:, k * hidden : (k + 1) * hidden].astype(ref.dtype)


def slice_grads(which, recv, weights, dtype):
    messages, slots, columns = recv.shape
    shape = weights[0].shape
    _, width, hidden = shape
    count = len(weights) // 2
    rows = messages * slots
    local = pl.BlockSpec(memory_space=pltpu.VMEM)
    anywhere = pl.BlockSpec(memory_space=pl.ANY)
    return pl.pallas_call(
        functools.partial(slices_kernel, count),
        in_specs=[pl.BlockSpec(memory_space=pltpu.SMEM), local] + [anywhere] * len(weights),
        out_specs=[local] * len(weights),
        out_shape=[jax.ShapeDtypeStruct(shape, dtype)] * len(weights),
        scratch_shapes=[
            pltpu.VMEM((rows, columns), recv.dtype),
            pltpu.VMEM((count, width, 2 * hidden), recv.dtype),
            pltpu.VMEM((rows, 2 * count * hidden), recv.dtype),
            pltpu.SemaphoreType.DMA((2 * count,)),
        ],
        compiler_params=pltpu.CompilerParams(vmem_limit_bytes=SLICE_VMEM),
        cost_estimate=pl.CostEstimate(
            flops=32 * rows * count * width * hidden,
            bytes_accessed=2 * recv.size + 8 * count * width * hidden,
            transcendentals=0,
        ),
        name="slice_grads",
    )(which, recv, *weights)


def moved(block, distance):
    planes = lax.axis_size("x")
    return lax.ppermute(block, "x", [(i, (i + distance) % planes) for i in range(planes)])


def add(*blocks):
    return sum(block.astype(jnp.float32) for block in blocks)


def body(tokens, expert_ids, gate_probs, act_grad, hot_experts, w_gate, w_up):
    width = tokens.shape[1]
    ff = act_grad.shape[2]
    copies = lax.axis_size("yh")
    experts = lax.axis_size(EXPERT)
    planes = lax.axis_size("x")
    here = lax.axis_index("x")
    anywhere = pl.BlockSpec(memory_space=pl.ANY)
    block, top, _ = act_grad.shape
    vmem = lambda *shape: pltpu.VMEM(shape, jnp.bfloat16)
    send = pl.pallas_call(
        pack_kernel,
        in_specs=[anywhere] * 5,
        out_specs=anywhere,
        out_shape=jax.ShapeDtypeStruct(
            (copies * experts, SLOTS, width + ff // copies), jnp.bfloat16
        ),
        scratch_shapes=[
            pltpu.VMEM((top, block), jnp.int32),
            pltpu.VMEM((1, hot_experts.size), jnp.int32),
            vmem(block, width),
            vmem(top, block, ff),
            pltpu.VMEM((top, block), jnp.float32),
            vmem(experts, SLOTS, width),
            vmem(copies * experts, SLOTS, ff // copies),
            pltpu.SemaphoreType.DMA((4 + top,)),
            pltpu.SemaphoreType.DMA((PIECES + 1, copies)),
        ],
        compiler_params=pltpu.CompilerParams(vmem_limit_bytes=VMEM),
        name="pack_rows",
    )(
        expert_ids.T,
        hot_experts.reshape(1, -1),
        tokens,
        jnp.swapaxes(act_grad, 0, 1),
        gate_probs.T,
    )
    send, w_gate, w_up = lax.optimization_barrier((send, w_gate, w_up))
    recv = lax.all_to_all(send, PLANE, 0, 0, tiled=True)
    mine = (w_gate, w_up)
    theirs = {d: tuple(moved(w, -d) for w in mine) for d in (2, 1, 3)}
    at = jnp.stack([(here + d) % planes for d in range(planes)])

    recv, theirs = lax.optimization_barrier((recv, theirs))
    far_gate, far_up = slice_grads(at[2:3], recv, theirs[2], jnp.bfloat16)
    far_gate_in = moved(far_gate, 1)
    far_up_in = moved(far_up, -1)
    right_gate, right_up, left_gate, left_up = slice_grads(
        at[1::2], recv, theirs[1] + theirs[3], jnp.bfloat16
    )
    from_left_up = moved(right_up, 1)
    from_right_gate = moved(left_gate, -1)
    sum_gate = add(right_gate, far_gate_in).astype(jnp.bfloat16)
    from_left_gate = moved(sum_gate, 1)
    sum_up = add(left_up, far_up_in).astype(jnp.bfloat16)
    from_right_up = moved(sum_up, -1)
    recv, _, _ = lax.optimization_barrier((recv, sum_gate, sum_up))
    own_gate, own_up = slice_grads(at[0:1], recv, mine, jnp.float32)
    own_gate, own_up, from_left_up, from_right_gate = lax.optimization_barrier(
        (own_gate, own_up, from_left_up, from_right_gate)
    )
    grad_gate = add(own_gate, from_right_gate, from_left_gate)
    grad_up = add(own_up, from_left_up, from_right_up)
    return (grad_gate.astype(jnp.bfloat16), grad_up.astype(jnp.bfloat16))


def solution(mesh):
    grid = Mesh(mesh.devices.reshape(2, 4, 4, 8, 2), AXES)
    rows = P(AXES)
    weights = P(EXPERT, None, ("yh", "x"))
    return jax.shard_map(
        body,
        mesh=grid,
        in_specs=(rows, rows, rows, rows, P(), weights, weights),
        out_specs=(weights, weights),
        check_vma=False,
    )
```

```python
import functools

import jax
import jax.numpy as jnp
from jax import lax
from jax.experimental import pallas as pl
from jax.experimental.pallas import tpu as pltpu
from jax.sharding import Mesh, PartitionSpec as P

CAP = 2
PIECES = 2
OVF = 2
SLOTS = CAP + OVF
VMEM = 60 * 2**20
SLICE_VMEM = 36 * 2**20
AXES = ("yh", "x", "yl", "z", "c")
PLANE = ("yh", "yl", "z", "c")
EXPERT = ("yl", "z", "c")


def pack_kernel(ids_hbm, hot_hbm, tok_hbm, act_hbm, probs_hbm, out_hbm, *scratch):
    ids_ref, hot_ref, tok_ref, act_ref, probs_ref, toks, acts, in_sems, out_sems = scratch
    top, block = ids_ref.shape
    experts = toks.shape[0]
    rows = experts * SLOTS
    width = tok_ref.shape[1]
    half = acts.shape[2]
    pairs = [(ids_hbm, ids_ref), (hot_hbm, hot_ref), (tok_hbm, tok_ref), (probs_hbm, probs_ref)]
    pairs += [(act_hbm.at[k], act_ref.at[k]) for k in range(top)]
    loads = [pltpu.make_async_copy(*pair, in_sems.at[i]) for i, pair in enumerate(pairs)]
    for load in loads:
        load.start()
    loads[0].wait()
    row = lax.broadcasted_iota(jnp.int32, (rows, block), 0)
    expert, slot = row // SLOTS, row % SLOTS
    hits = [ids_ref[k : k + 1, :] == expert for k in range(top)]
    named = hits[0]
    for hit in hits[1:]:
        named = named | hit
    before = lax.broadcasted_iota(jnp.int32, (block, block), 0) < lax.broadcasted_iota(
        jnp.int32, (block, block), 1
    )
    position = jnp.dot(
        jnp.where(named, 1.0, 0.0).astype(jnp.bfloat16),
        jnp.where(before, 1.0, 0.0).astype(jnp.bfloat16),
        preferred_element_type=jnp.float32,
    ).astype(jnp.int32)
    loads[1].wait()
    hots = hot_ref.shape[1]
    owner = lax.broadcasted_iota(jnp.int32, (rows, hots), 0) // SLOTS
    hot = jnp.max(jnp.where(hot_ref[...] == owner, 1, 0), axis=1, keepdims=True)
    kept = named & (position == slot) & ((slot < CAP) | (hot > 0))
    pick = jnp.where(kept, 1.0, 0.0).astype(jnp.bfloat16)
    sends = []
    loads[2].wait()
    piece = width // PIECES
    for p in range(PIECES):
        cols = slice(p * piece, (p + 1) * piece)
        got = jnp.dot(pick, tok_ref[:, cols], preferred_element_type=jnp.float32)
        toks[:, :, cols] = got.astype(jnp.bfloat16).reshape(experts, SLOTS, piece)
        for copy in range(2):
            part = (pl.ds(copy * experts, experts), slice(None), pl.ds(p * piece, piece))
            sends.append(
                pltpu.make_async_copy(
                    toks.at[:, :, pl.ds(p * piece, piece)], out_hbm.at[part], out_sems.at[p, copy]
                )
            )
            sends[-1].start()
    total = jnp.zeros((rows, act_ref.shape[2]), jnp.float32)
    scale = jnp.zeros((rows, block), jnp.float32)
    loads[3].wait()
    for k in range(top):
        loads[4 + k].wait()
        chosen = jnp.where(kept & hits[k], 1.0, 0.0)
        total += jnp.dot(chosen.astype(jnp.bfloat16), act_ref[k], preferred_element_type=jnp.float32)
        scale += chosen * probs_ref[k : k + 1, :]
    total = (jnp.sum(scale, axis=1, keepdims=True) * total).astype(jnp.bfloat16)
    for copy in range(2):
        here = slice(copy * experts, (copy + 1) * experts)
        acts[here] = total[:, copy * half : (copy + 1) * half].reshape(experts, SLOTS, half)
    sends.append(
        pltpu.make_async_copy(acts, out_hbm.at[:, :, pl.ds(width, half)], out_sems.at[PIECES, 0])
    )
    sends[-1].start()
    for send in sends:
        send.wait()


def pre_grads(gate, up, act):
    upstream = act.astype(jnp.float32)
    sig = 1.0 / (1.0 + jnp.exp(-gate))
    d_up = upstream * gate * sig
    d_gate = upstream * up * sig * (1.0 + gate * (1.0 - sig))
    return [d_gate.astype(jnp.bfloat16), d_up.astype(jnp.bfloat16)]


CHUNKS = 1
TILES = 5


def slices_kernel(count, which_ref, recv_ref, *refs):
    weights_hbm, grads = refs[: 2 * count], refs[2 * count : 4 * count]
    rows, weights, d, sems = refs[4 * count :]
    width, hidden = weights_hbm[0].shape[1:]
    loads = [
        pltpu.make_async_copy(
            source.at[0], weights.at[j // 2, :, pl.ds(j % 2 * hidden, hidden)], sems.at[j]
        )
        for j, source in enumerate(weights_hbm)
    ]
    for load in loads:
        load.start()
    messages = recv_ref.shape[0] // CHUNKS
    chunk = messages * SLOTS
    for c in range(CHUNKS):
        got = recv_ref[c * messages : (c + 1) * messages]
        rows[c * chunk : (c + 1) * chunk, :] = got.reshape(chunk, rows.shape[1])
    for k in range(count):
        for load in loads[2 * k : 2 * k + 2]:
            load.wait()
        start = pl.multiple_of(width + which_ref[k] * hidden, hidden)
        for c in range(CHUNKS):
            part = slice(c * chunk, (c + 1) * chunk)
            both = jnp.dot(rows[part, :width], weights[k], preferred_element_type=jnp.float32)
            upstream = rows[part, pl.ds(start, hidden)]
            d_gate, d_up = pre_grads(both[:, :hidden], both[:, hidden:], upstream)
            d[part, 2 * k * hidden : (2 * k + 1) * hidden] = d_gate
            d[part, (2 * k + 1) * hidden : (2 * k + 2) * hidden] = d_up
    tile = width // TILES
    for t in range(TILES):
        cols = slice(t * tile, (t + 1) * tile)
        total = lax.dot_general(
            rows[:, cols], d[...], (((0,), (0,)), ((), ())), preferred_element_type=jnp.float32
        )
        for k, ref in enumerate(grads):
            ref[0, cols, :] = total[:, k * hidden : (k + 1) * hidden].astype(ref.dtype)


def slice_grads(which, recv, weights, dtype):
    messages, slots, columns = recv.shape
    shape = weights[0].shape
    _, width, hidden = shape
    count = len(weights) // 2
    rows = messages * slots
    local = pl.BlockSpec(memory_space=pltpu.VMEM)
    anywhere = pl.BlockSpec(memory_space=pl.ANY)
    return pl.pallas_call(
        functools.partial(slices_kernel, count),
        in_specs=[pl.BlockSpec(memory_space=pltpu.SMEM), local] + [anywhere] * len(weights),
        out_specs=[local] * len(weights),
        out_shape=[jax.ShapeDtypeStruct(shape, dtype)] * len(weights),
        scratch_shapes=[
            pltpu.VMEM((rows, columns), recv.dtype),
            pltpu.VMEM((count, width, 2 * hidden), recv.dtype),
            pltpu.VMEM((rows, 2 * count * hidden), recv.dtype),
            pltpu.SemaphoreType.DMA((2 * count,)),
        ],
        compiler_params=pltpu.CompilerParams(vmem_limit_bytes=SLICE_VMEM),
        cost_estimate=pl.CostEstimate(
            flops=32 * rows * count * width * hidden,
            bytes_accessed=2 * recv.size + 8 * count * width * hidden,
            transcendentals=0,
        ),
        name="slice_grads",
    )(which, recv, *weights)


def moved(block, distance):
    planes = lax.axis_size("x")
    return lax.ppermute(block, "x", [(i, (i + distance) % planes) for i in range(planes)])


def add(*blocks):
    return sum(block.astype(jnp.float32) for block in blocks)


def body(tokens, expert_ids, gate_probs, act_grad, hot_experts, w_gate, w_up):
    width = tokens.shape[1]
    ff = act_grad.shape[2]
    copies = lax.axis_size("yh")
    experts = lax.axis_size(EXPERT)
    planes = lax.axis_size("x")
    here = lax.axis_index("x")
    anywhere = pl.BlockSpec(memory_space=pl.ANY)
    block, top, _ = act_grad.shape
    vmem = lambda *shape: pltpu.VMEM(shape, jnp.bfloat16)
    send = pl.pallas_call(
        pack_kernel,
        in_specs=[anywhere] * 5,
        out_specs=anywhere,
        out_shape=jax.ShapeDtypeStruct(
            (copies * experts, SLOTS, width + ff // copies), jnp.bfloat16
        ),
        scratch_shapes=[
            pltpu.VMEM((top, block), jnp.int32),
            pltpu.VMEM((1, hot_experts.size), jnp.int32),
            vmem(block, width),
            vmem(top, block, ff),
            pltpu.VMEM((top, block), jnp.float32),
            vmem(experts, SLOTS, width),
            vmem(copies * experts, SLOTS, ff // copies),
            pltpu.SemaphoreType.DMA((4 + top,)),
            pltpu.SemaphoreType.DMA((PIECES + 1, copies)),
        ],
        compiler_params=pltpu.CompilerParams(vmem_limit_bytes=VMEM),
        name="pack_rows",
    )(
        expert_ids.T,
        hot_experts.reshape(1, -1),
        tokens,
        jnp.swapaxes(act_grad, 0, 1),
        gate_probs.T,
    )
    send, w_gate, w_up = lax.optimization_barrier((send, w_gate, w_up))
    recv = lax.all_to_all(send, PLANE, 0, 0, tiled=True)
    mine = (w_gate, w_up)
    theirs = {d: tuple(moved(w, -d) for w in mine) for d in (2, 1, 3)}
    at = jnp.stack([(here + d) % planes for d in range(planes)])

    recv, theirs = lax.optimization_barrier((recv, theirs))
    far_gate, far_up = slice_grads(at[2:3], recv, theirs[2], jnp.bfloat16)
    far_gate_in = moved(far_gate, 1)
    far_up_in = moved(far_up, -1)
    right_gate, right_up, left_gate, left_up = slice_grads(
        at[1::2], recv, theirs[1] + theirs[3], jnp.bfloat16
    )
    from_left_up = moved(right_up, 1)
    from_right_gate = moved(left_gate, -1)
    sum_gate = add(right_gate, far_gate_in).astype(jnp.bfloat16)
    from_left_gate = moved(sum_gate, 1)
    sum_up = add(left_up, far_up_in).astype(jnp.bfloat16)
    from_right_up = moved(sum_up, -1)
    recv, _, _ = lax.optimization_barrier((recv, sum_gate, sum_up))
    own_gate, own_up = slice_grads(at[0:1], recv, mine, jnp.float32)
    own_gate, own_up, from_left_up, from_right_gate = lax.optimization_barrier(
        (own_gate, own_up, from_left_up, from_right_gate)
    )
    grad_gate = add(own_gate, from_right_gate, from_left_gate)
    grad_up = add(own_up, from_left_up, from_right_up)
    return (grad_gate.astype(jnp.bfloat16), grad_up.astype(jnp.bfloat16))


def solution(mesh):
    grid = Mesh(mesh.devices.reshape(2, 4, 4, 8, 2), AXES)
    rows = P(AXES)
    weights = P(EXPERT, None, ("yh", "x"))
    return jax.shard_map(
        body,
        mesh=grid,
        in_specs=(rows, rows, rows, rows, P(), weights, weights),
        out_specs=(weights, weights),
        check_vma=False,
    )
```
